128 devices in a mesh: index: 16 (over y, x_hi, core), rep: 4 (over z), tp: 2 (over x_lo).
Axes of the slice: x: 4 (x_hi: 2, x_lo: 2; x = x_hi * 2 + x_lo), y: 4, z: 4, core: 2. Of those that a mesh axis runs over, the one named last changes fastest.
Arguments:
- queries: bfloat16 [2048, 1024], P(('index', 'rep', 'tp')), may hold values from -150 to 150
- passages: bfloat16 [32768, 1024], P('index'), may hold values from -30 to 30
- probe_owner: int32 [2048, 4], P(('index', 'rep', 'tp')), may hold values from 0 to 15, all different within a row; in each aligned block of 16 rows (0 to 15, 16 to 31, ...) at most 8 rows name the same one
- probe_cluster: int32 [2048, 4], P(('index', 'rep', 'tp')), may hold values from 0 to 3
- pair_owner: int32 [2048, 64, 1], P(('index', 'rep', 'tp')), may hold values from 0 to 15; in each aligned block of 1024 rows (0 to 1023, 1024 to 2047, ..., all dimensions but the last counted through in order) at most 128 rows name the same one
- pair_row: int32 [2048, 64], P(('index', 'rep', 'tp')), may hold values from 0 to 2047
- w_qkv: bfloat16 [1024, 3, 1024], P(None, None, 'tp'), may hold values from -0.046875 to 0.046875
- w_out: bfloat16 [1024, 1024], P('tp'), may hold values from -0.375 to 0.375
- w_up: bfloat16 [1024, 4096], P(None, 'tp'), may hold values from -0.1875 to 0.1875
- w_down: bfloat16 [4096, 1024], P('tp'), may hold values from -0.09375 to 0.09375
- gain_one: float32 [1024], replicated, may hold values from 0.1 to 1.9
- gain_two: float32 [1024], replicated, may hold values from 0.1 to 1.9
Outputs:
- reranked: bfloat16 [2048, 65, 1024], P(('index', 'rep', 'tp'))
The draws below stay inside these ranges and needn't reach their ends.
Inputs may be any that keep to these rules, and one draw needn't show every extreme that they name: `probe_owner`: each query names 4 different owners; within the queries of one device (aligned blocks of 16 queries) no owner is named more than 8 times, a bound that some block reaches. `pair_owner`: within the candidates of one device (aligned blocks of 1024) no owner is named more than 128 times, a bound that some block reaches.
All inputs are finite; a program needn't handle non-finite values.
Results may differ from the reference program's by a relative error of at most 0.013.
Values may be sent and summed in bfloat16 or wider, within the bound.
A program may use at most 192 MiB of HBM per device.

```python
import math
import jax
import jax.numpy as jnp
import numpy as np
from jax import lax

D = 1024
HEADS = 16
HD = 64
FF = 4096
K = 64
NPROBE = 4
CL_DEV = 4
CL_ROWS = 512
Q_DEV = 16
S = 65
PASS_DEV = 2048
PASSAGES = 32768
QUERIES = 2048
CAP = 8
FCAP = 128
N_INDEX = 16


def draw_queries(key, part):
    key = jax.random.fold_in(key, 11)
    first_key = jax.random.fold_in(key, 0)
    values = 0.45 * jax.random.truncated_normal(first_key, -6.0, 6.0, (QUERIES, D), jnp.float32)
    return values.astype(jnp.bfloat16)


def draw_passages(key, part):
    key = jax.random.fold_in(key, 12)
    first_key = jax.random.fold_in(key, 0)
    values = 4.0 * jax.random.truncated_normal(first_key, -6.0, 6.0, (PASSAGES, D), jnp.float32)
    return values.astype(jnp.bfloat16)


def touch_ends(array, key, least, top_value):
    place = [jax.random.randint(jax.random.fold_in(key, axis), (), 0, length) for axis, length in enumerate(array.shape)]
    main_axis = array.shape.index(max(array.shape))
    beside = place[:main_axis] + [(place[main_axis] + 1) % array.shape[main_axis]] + place[main_axis + 1:]
    return array.at[tuple(place)].set(least).at[tuple(beside)].set(top_value)


def shard_levels(key, dims, cuts, least, largest):
    gain, own = 1.0, jax.random.fold_in(key, 6)
    for axis_at, shards_of in cuts:
        heights = jnp.exp(jax.random.uniform(jax.random.fold_in(own, axis_at), (shards_of,), jnp.float32, least / len(cuts), largest / len(cuts)))
        gain = gain * jnp.repeat(heights, dims[axis_at] // shards_of).reshape([-1 if axis == axis_at else 1 for axis in range(len(dims))])
    return gain


def assign_block(rng, own, number, rows, count, top, most, lean):
    order = jax.random.permutation(rng, count)
    heavy_load, ordinary = shares(count, rows * top, most, lean, True), shares(count, rows * top, most, lean, False)
    places = jnp.arange(count)

    def named(lengths, turn):
        used = int((lengths > 0).sum())
        fixed = max(1, used // 4)
        moved = fixed + (places - fixed + turn * (used - fixed)) % max(1, count - fixed)
        return jnp.zeros((count,), jnp.int32).at[order[jnp.where(places < fixed, places, moved)]].set(jnp.asarray(lengths, jnp.int32))

    lengths = jnp.where(number % 4 == 0, named(heavy_load, number // 4), named(ordinary, number - number // 4 - 1))
    mixed = jax.random.permutation(jax.random.fold_in(own, 3), count)
    donor, receiver = mixed[0:count // 2 * 2:2], mixed[1:count // 2 * 2:2]
    slack = jnp.minimum(lengths[donor] - 1, most - lengths[receiver]) // 2
    slack = jnp.where((donor == order[0]) | (receiver == order[0]) | (lengths[receiver] == 0), 0, jnp.maximum(slack, 0))
    moved = jax.random.randint(jax.random.fold_in(own, 4), (count // 2,), 0, 1 << 20) % (slack + 1)
    lengths = lengths.at[donor].add(-moved).at[receiver].add(moved)
    items = jnp.searchsorted(jnp.cumsum(lengths), jnp.arange(rows * top), side="right").astype(jnp.int32)
    listing = items.reshape(top, rows).T
    listing = listing[jax.random.permutation(jax.random.fold_in(own, 1), rows)]
    turn = jax.random.randint(jax.random.fold_in(own, 2), (rows, 1), 0, top)
    return jnp.take_along_axis(listing, (jnp.arange(top)[None, :] + turn) % top, axis=1)


def shares(count, total, most, skew, full):
    weights = [(1 << 20) // math.isqrt(rank ** skew) + 1 for rank in range(1, count + 1)]
    largest = most if full else min(most, max(-(-total // count), total * weights[0] // sum(weights)))
    least = 1 if total - largest >= count - 1 else 0
    given, surplus = [largest] + [least] * (count - 1), total - largest - least * (count - 1)
    while surplus > 0:
        free = [i for i in range(1, count) if given[i] < largest] or [i for i in range(1, count) if given[i] < most]
        pool, left = sum([weights[i] for i in free]), surplus
        for i in free:
            extra = min(most - given[i], max(1, left * weights[i] // pool), surplus)
            given[i] = given[i] + extra
            surplus = surplus - extra
    return np.array(given)


def scatter_about(own_key, dims, scale, reach, shards=(), kind=jnp.bfloat16):
    entries = scale * jax.random.normal(own_key, dims, jnp.float32)
    if shards:
        entries = entries * shard_levels(own_key, dims, shards, -0.22, 0.18)
    return jnp.clip(entries, -reach, reach).astype(kind)


def setup_inputs(seed: int = 0) -> dict:
    arg_keys = jax.random.split(jax.random.key(seed), 13)
    queries = draw_queries(jax.random.fold_in(arg_keys[12], 71), 0)
    passages = draw_passages(jax.random.fold_in(arg_keys[12], 71), 0)
    probe_owner_keys = jax.random.split(jax.random.fold_in(arg_keys[2], 1), QUERIES // Q_DEV)
    probe_owner_turns = jax.random.permutation(jax.random.fold_in(arg_keys[2], 3), QUERIES // Q_DEV)
    probe_owner = jax.vmap(lambda own, number: assign_block(jax.random.fold_in(arg_keys[2], 2), own, number, Q_DEV, N_INDEX, NPROBE, CAP, 2))(probe_owner_keys, probe_owner_turns).reshape((QUERIES, NPROBE))
    probe_cluster = touch_ends(jax.random.randint(arg_keys[3], (QUERIES, NPROBE), 0, CL_DEV), jax.random.fold_in(arg_keys[3], 1), 0, CL_DEV - 1).astype(jnp.int32)
    pair_owner_keys = jax.random.split(jax.random.fold_in(arg_keys[4], 1), QUERIES * K // (Q_DEV * K))
    pair_owner_turns = jax.random.permutation(jax.random.fold_in(arg_keys[4], 3), QUERIES * K // (Q_DEV * K))
    pair_owner = jax.vmap(lambda own, number: assign_block(jax.random.fold_in(arg_keys[4], 2), own, number, Q_DEV * K, N_INDEX, 1, FCAP, 2))(pair_owner_keys, pair_owner_turns).reshape((QUERIES, K, 1))
    pair_row = touch_ends(jax.random.randint(arg_keys[5], (QUERIES, K), 0, PASS_DEV), jax.random.fold_in(arg_keys[5], 1), 0, PASS_DEV - 1).astype(jnp.int32)
    w_qkv = scatter_about(arg_keys[6], (D, 3, D), (16 * D) ** -0.5, 0.046875, ((2, 2),))
    w_out = scatter_about(arg_keys[7], (D, D), (D // 4) ** -0.5, 0.375, ((0, 2),))
    w_up = scatter_about(arg_keys[8], (D, FF), D ** -0.5, 0.1875, ((1, 2),))
    w_down = scatter_about(arg_keys[9], (FF, D), FF ** -0.5, 0.09375, ((0, 2),))
    gain_one = jnp.clip(1.0 + 0.18 * jax.random.normal(arg_keys[10], (D,), jnp.float32), 0.1, 1.9)
    gain_two = jnp.clip(1.0 + 0.18 * jax.random.normal(arg_keys[11], (D,), jnp.float32), 0.1, 1.9)
    return dict(queries=queries, passages=passages, probe_owner=probe_owner, probe_cluster=probe_cluster, pair_owner=pair_owner, pair_row=pair_row, w_qkv=w_qkv, w_out=w_out, w_up=w_up, w_down=w_down, gain_one=gain_one, gain_two=gain_two)


def layer_norm(values, scale_gain):
    center_mean = lax.optimization_barrier(jnp.mean(values, -1, keepdims=True))
    centered = values - center_mean
    variance = lax.optimization_barrier(jnp.mean(centered * centered, -1, keepdims=True))
    return centered * lax.rsqrt(variance + 1e-05) * scale_gain

def encode(block, w_qkv, w_out, w_up, w_down, gain_one, gain_two):
    f32 = jnp.float32
    count = block.shape[0]
    qkv = jnp.einsum('bsd,dcf->bscf', block.astype(f32), w_qkv.astype(f32)).astype(jnp.bfloat16)
    qkv = qkv.reshape(count, S, 3, HEADS, HD)
    query_part = qkv[:, :, 0].astype(f32)
    key_part = qkv[:, :, 1].astype(f32)
    value_part = qkv[:, :, 2].astype(f32)
    scores = jnp.einsum('bshe,bthe->bhst', query_part, key_part) * HD ** (-0.5)
    probs = jax.nn.softmax(scores, -1).astype(jnp.bfloat16)
    context = jnp.einsum('bhst,bthe->bshe', probs.astype(f32), value_part).astype(jnp.bfloat16)
    context = context.reshape(count, S, D)
    attn = jnp.einsum('bsf,fd->bsd', context.astype(f32), w_out.astype(f32))
    hidden = layer_norm(block.astype(f32) + attn, gain_one).astype(jnp.bfloat16)
    active = jax.nn.gelu(jnp.einsum('bsd,df->bsf', hidden.astype(f32), w_up.astype(f32)), approximate=False).astype(jnp.bfloat16)
    down = jnp.einsum('bsf,fd->bsd', active.astype(f32), w_down.astype(f32))
    return layer_norm(hidden.astype(f32) + down, gain_two).astype(jnp.bfloat16)

def reference(queries, passages, probe_owner, probe_cluster, pair_owner, pair_row, w_qkv, w_out, w_up, w_down, gain_one, gain_two):
    f32 = jnp.float32
    clusters = passages.reshape(N_INDEX * CL_DEV, CL_ROWS, D)
    target = probe_owner * CL_DEV + probe_cluster
    query_float = queries.astype(f32)
    inverse = D ** (-0.5)

    def visit(total, item):
        number, members = item
        member_float = members.astype(f32)
        scores = jnp.dot(query_float, member_float.T) * inverse
        weights = jax.nn.softmax(scores, -1).astype(jnp.bfloat16)
        pooled = jnp.dot(weights.astype(f32), member_float).astype(jnp.bfloat16)
        hits = lax.optimization_barrier(jnp.sum((target == number).astype(f32), 1, keepdims=True))
        return (total + hits * pooled.astype(f32), None)
    numbers = jnp.arange(N_INDEX * CL_DEV, dtype=jnp.int32)
    total, _ = lax.scan(visit, jnp.zeros((QUERIES, D), f32), (numbers, clusters))
    retrieval = total / NPROBE
    lead = (query_float + retrieval).astype(jnp.bfloat16)
    pair_ids = (pair_owner[:, :, 0] * PASS_DEV + pair_row).astype(jnp.int32)
    candidates = jnp.take(passages, pair_ids, axis=0)
    tokens = jnp.concatenate([lead[:, None, :], candidates], 1)
    blocks = tokens.reshape(QUERIES // Q_DEV, Q_DEV, S, D)
    result = lax.map(lambda block: encode(block, w_qkv, w_out, w_up, w_down, gain_one, gain_two), blocks)
    return result.reshape(QUERIES, S, D)
```

```python
import math

import jax
import jax.numpy as jnp
from jax import lax
from jax.experimental import pallas as pl
from jax.experimental.pallas import tpu as pltpu
from jax.sharding import PartitionSpec as P

NT = (((1,), (1,)), ((), ()))
MESH = pl.DeviceIdType.MESH
bf16 = jnp.bfloat16
f32 = jnp.float32
D = 1024
Q_DEV = 16
PASS_DEV = 2048
N_C = 1024
N_TOK = 1040

def gelu(x):
    ax=jnp.abs(x)
    t=1.0/(1.0+(0.3275911*math.sqrt(0.5))*ax)
    e=jnp.exp2((-0.5/math.log(2.0))*(x*x))
    p=0.5*0.254829592+t*(0.5*-0.284496736+t*(0.5*1.421413741+t*(0.5*-1.453152027+t*(0.5*1.061405429))))
    return jnp.maximum(x,0.0)-ax*(p*t*e)

def norm(v,g):
    c=v-jnp.mean(v,-1,keepdims=True)
    var=jnp.mean(c*c,-1,keepdims=True)
    return c*lax.rsqrt(var+1e-5)*g

def layer_kernel(tok,wq0,wq1,wo0,wo1,wu0,wu1,wd0,wd1,g1,g2,out,
                 wq,wo,wu,wd,q,k,v,kl,vl,ctx,ctxl,acc,sems):
    cps=[]
    for n,(dst,a,b) in enumerate(((wq,wq0,wq1),(wo,wo0,wo1),(wu,wu0,wu1),(wd,wd0,wd1))):
        for s,src in enumerate((a,b)):
            c=pltpu.make_async_copy(src,dst.at[s],sems.at[n,s]); c.start(); cps.append(c)
    for i in range(2):
        cps[i].wait()
        def qkv_step(n,carry):
            col=pl.ds(pl.multiple_of(n*256,256),256)
            ocol=pl.ds(pl.multiple_of(i*512+n*256,256),256)
            for j,ref in enumerate((q,k,v)):
                r=jnp.dot(tok[...],wq[i,j,:,col],preferred_element_type=f32)
                if j==0: r=r*0.125
                ref[:,ocol]=r.astype(bf16)
            return carry
        lax.fori_loop(0,2,qkv_step,0)
    kl[...]=k[N_C:,:].astype(f32); vl[...]=v[N_C:,:].astype(f32)
    ctxl[...]=jnp.zeros_like(ctxl)
    lane=lax.broadcasted_iota(jnp.int32,(64,256),1)//64
    ones_bd=(lax.broadcasted_iota(jnp.int32,(256,256),0)//64==lax.broadcasted_iota(jnp.int32,(256,256),1)//64).astype(bf16)
    low=lax.broadcasted_iota(jnp.int32,(80,128),1)<64
    rowid=lax.broadcasted_iota(jnp.int32,(16,256),0)
    def bd(x):
        return jnp.concatenate([jnp.where(lane==h,x,jnp.zeros_like(x)) for h in range(4)],0)
    def att(g,carry):
        rows=pl.ds(pl.multiple_of(g*64,64),64)
        es=[];els=[];
        for j in range(4):
            cs=slice(j*256,(j+1)*256)
            Q=jnp.concatenate([q[rows,cs],q[N_C:,cs]],0)
            klb=jnp.broadcast_to(kl[pl.ds(g,1),cs],(64,256)).astype(bf16)
            S=lax.dot_general(Q,bd(k[rows,cs]),NT,preferred_element_type=f32)
            SL=lax.dot_general(Q,bd(klb),NT,preferred_element_type=f32)
            ms=[]
            for b in range(2):
                X=S[:,b*128:(b+1)*128]
                mA=jnp.max(jnp.where(low,X,-jnp.inf),1,keepdims=True)
                mB=jnp.max(jnp.where(low,-jnp.inf,X),1,keepdims=True)
                ms.append(jnp.where(low,mA,mB))
            m=jnp.maximum(jnp.concatenate(ms,1),SL)
            es.append(jnp.exp(S-m).astype(bf16)); els.append(jnp.exp(SL-m))
        den=jnp.dot(jnp.concatenate(es,0),ones_bd,preferred_element_type=f32)
        for j in range(4):
            cs=slice(j*256,(j+1)*256)
            pv=jnp.dot(es[j],bd(v[rows,cs]),preferred_element_type=f32)
            c=(pv+els[j]*vl[pl.ds(g,1),cs])/(den[j*80:(j+1)*80]+els[j])
            ctx[rows,cs]=c[:64].astype(bf16)
            ctxl[:,cs]+=jnp.where(rowid==g,c[64:],0.0)
        return carry
    lax.fori_loop(0,16,att,0)
    ctx[N_C:,:]=ctxl[...].astype(bf16)
    cps[2].wait(); cps[3].wait()
    def outp(rows,n):
        a=jnp.dot(ctx[rows,:512],wo[0],preferred_element_type=f32)+jnp.dot(ctx[rows,512:],wo[1],preferred_element_type=f32)
        return norm(tok[rows,:].astype(f32)+a,g1[...]).astype(bf16).astype(f32)
    def put(g,y):
        for c in range(8): acc[c,pl.ds(16+g,64,stride=16),:]=y[:,c*128:(c+1)*128]
    def outc(i,carry):
        h=outp(pl.ds(pl.multiple_of(i*256,256),256),256)
        for l in range(4):
            put(i*4+l,h[l*64:(l+1)*64])
        return carry
    lax.fori_loop(0,3,outc,0)
    h=outp(slice(768,1040),272)
    for l in range(4):
        put(12+l,h[l*64:(l+1)*64])
    for c in range(8): acc[c,0:16,:]=h[256:,c*128:(c+1)*128]
    for c in cps[4:]: c.wait()
    def ffn(r,carry):
        rows=pl.ds(pl.multiple_of(r*208,16),208)
        t=jnp.concatenate([acc[c,rows,:] for c in range(8)],1)
        x=t.astype(bf16)
        acts=[]
        for i in range(2):
            for n in range(4):
                u=jnp.dot(x,wu[i,:,n*512:(n+1)*512],preferred_element_type=f32)
                acts.append(gelu(u).astype(bf16))
        for i in range(2):
            t=t+jnp.dot(jnp.concatenate(acts[i*4:(i+1)*4],1),wd[i],preferred_element_type=f32)
        out[rows,:]=norm(t,g2[...]).astype(bf16)
        return carry
    lax.fori_loop(0,5,ffn,0)

def layer(tok,wq0,wq1,wo0,wo1,wu0,wu1,wd0,wd1,g1,g2):
    V=pl.BlockSpec(memory_space=pltpu.VMEM); A=pl.BlockSpec(memory_space=pl.ANY)
    o=pl.pallas_call(layer_kernel,out_shape=jax.ShapeDtypeStruct((N_TOK,D),bf16),
        in_specs=[V]+[A]*8+[V,V],out_specs=V,
        scratch_shapes=[pltpu.VMEM((2,3,1024,512),bf16),pltpu.VMEM((2,512,1024),bf16),pltpu.VMEM((2,1024,2048),bf16),pltpu.VMEM((2,2048,1024),bf16),
          pltpu.VMEM((N_TOK,D),bf16),pltpu.VMEM((N_TOK,D),bf16),pltpu.VMEM((N_TOK,D),bf16),pltpu.VMEM((16,D),f32),pltpu.VMEM((16,D),f32),
          pltpu.VMEM((N_TOK,D),bf16),pltpu.VMEM((16,D),f32),pltpu.VMEM((8,N_TOK,128),f32),pltpu.SemaphoreType.DMA((4,2))],
        compiler_params=pltpu.CompilerParams(vmem_limit_bytes=60*2**20),name="layer",
        cost_estimate=pl.CostEstimate(flops=2*1040*12*2**20,bytes_accessed=30*2**20,transcendentals=8*2**20))(tok,wq0,wq1,wo0,wo1,wu0,wu1,wd0,wd1,g1,g2)
    return jnp.transpose(o.reshape(65,16,D),(1,0,2))

ORDER = ((2, 1), (2, 0), (1, 1), (3, 1), (1, 0), (3, 0), (0, 1), (0, 0))
UNITS = ((0, 0), (0, 1), (0, 2), (1, 0), (2, 0), (3, 0))
ROWS = (128, 64, 128, 256)


def inverse(k):
    return ((4 - k // 4) % 4) * 4 + k % 4


def front_kernel(
    own,
    pay,
    qry,
    psg_in,
    wq_i,
    wo_i,
    wu_i,
    wd_i,
    tok,
    wq_o,
    wo_o,
    wu_o,
    wd_o,
    psg,
    qall,
    msg,
    got,
    hot,
    reply,
    back,
    codes,
    frows,
    score,
    pool,
    prow,
    flatcol,
    psem,
    qsem,
    msem,
    rsem,
    osem,
    wsend,
    wrecv,
):
    idx = lax.axis_index("index")
    z = lax.axis_index("rep")
    t = lax.axis_index("tp")
    y, xh, c = idx // 4, (idx // 2) % 2, idx % 2

    def peer(k):
        dy, dx, dc = k // 4, (k // 2) % 2, k % 2
        return (((y + dy) % 4) * 4 + ((xh + dx) % 2) * 2 + (c + dc) % 2, z, (t + dx) % 2)

    partner = (idx, z, 1 - t)
    z_up = (idx, (z + 1) % 4, t)
    z_down = (idx, (z + 3) % 4, t)
    barrier = pltpu.get_barrier_semaphore()
    for device in [peer(k) for k in range(1, 16)] + [partner, z_up, z_down]:
        pl.semaphore_signal(barrier, inc=1, device_id=device, device_id_type=MESH)
    load = pltpu.make_async_copy(psg_in, psg, psem)
    load.start()

    owner = own[...]
    rel = (((owner >> 2) - y) & 3) * 4 + (((owner >> 1) & 1) ^ xh) * 2 + ((owner & 1) ^ c)
    rel = jnp.where(owner < 0, -1, rel).astype(f32)
    sub16 = lax.broadcasted_iota(jnp.int32, (16, 128), 0).astype(f32)
    marks = [jnp.where(rel[r : r + 1, :] == sub16, 1.0, 0.0) for r in range(16)]
    onehot = jnp.concatenate(marks, 0)
    onehot16 = onehot.astype(bf16)
    row128 = lax.broadcasted_iota(jnp.int32, (128, 128), 0)
    col128 = lax.broadcasted_iota(jnp.int32, (128, 128), 1)
    same = (row128 // 64) == (col128 // 64)
    earlier = jnp.where(same & (row128 < col128), 1.0, 0.0).astype(bf16)
    block = jnp.where(same, 1.0, 0.0).astype(bf16)
    row256 = lax.broadcasted_iota(jnp.int32, (256, 256), 0)
    col256 = lax.broadcasted_iota(jnp.int32, (256, 256), 1)
    above = jnp.where(((row256 % 16) == (col256 % 16)) & (col256 < row256 - row256 % 16), 1.0, 0.0)
    lists_before = jnp.dot(above.astype(bf16), onehot16, preferred_element_type=f32).astype(bf16)
    count = jnp.dot(onehot16, earlier, preferred_element_type=f32)
    count = count + jnp.dot(lists_before, block, preferred_element_type=f32)
    slot = jnp.sum((onehot * count).reshape(16, 16, 128), 1)

    lane16 = lax.broadcasted_iota(jnp.int32, (16, 128), 1)
    target = jnp.where(lane16 < 64, slot, slot + 128.0)
    high = (pay[...] >> 5).astype(f32)
    low = (pay[...] & 31).astype(f32)
    sub256 = lax.broadcasted_iota(jnp.int32, (256, 128), 0).astype(f32)
    pad = jnp.zeros((96, 128), f32)
    table = jnp.zeros((256, 128), f32)
    for r in range(16):
        here = jnp.where(target[r : r + 1, :] == sub256, 1.0, 0.0).astype(bf16)
        digit = jnp.concatenate([marks[r] * high[r : r + 1, :], marks[r] * low[r : r + 1, :], pad], 0)
        table = table + lax.dot_general(here, digit.astype(bf16), NT, preferred_element_type=f32)
    table = jnp.transpose(table)
    table = table[:16] * 32.0 + table[16:32]
    for k in range(16):
        msg[k] = jnp.broadcast_to(table[k : k + 1, :], (8, 256))
    got[0] = msg[0]
    qall[0] = qry[...]

    pl.semaphore_wait(barrier, 18)

    w_in = (wq_i, wo_i, wu_i, wd_i)
    w_out = (wq_o, wo_o, wu_o, wd_o)

    def share(refs, unit, zz, cc, half=None):
        n, j = UNITS[unit]
        rows = ROWS[n]
        start = (zz * 2 + cc) * rows
        if half is not None:
            rows = rows // 2
            start = start + half * rows
        part = pl.ds(pl.multiple_of(start, 32), rows)
        return refs[n].at[j, part, :] if n == 0 else refs[n].at[part, :]

    def push(src, dst, unit, s, device):
        copy = pltpu.make_async_remote_copy(
            src_ref=src,
            dst_ref=dst,
            send_sem=wsend.at[unit, s],
            recv_sem=wrecv.at[unit, s],
            device_id=device,
            device_id_type=MESH,
        )
        copy.start()
        return copy

    started = {}
    for u in range(6):
        started[u, 0] = push(share(w_in, u, z, c), share(w_out, u, z, c), u, 0, partner)

    def relay(u, stage):
        def put(s, zz, half, device):
            ref = share(w_out, u, zz, c, half)
            started[u, s] = push(ref, ref, u, s, device)

        zm, zp, zo = (z + 3) % 4, (z + 1) % 4, (z + 2) % 4
        if stage == 0:
            started[u, 0].wait_recv()
            put(1, z, None, z_up)
            put(2, z, None, z_down)
            put(5, z, None, peer(1))
        elif stage == 1:
            started[u, 1].wait_recv()
            put(3, zm, 0, z_up)
            put(6, zm, None, peer(1))
            started[u, 2].wait_recv()
            put(4, zp, 1, z_down)
            put(7, zp, None, peer(1))
        else:
            started[u, 3].wait_recv()
            started[u, 4].wait_recv()
            put(8, zo, None, peer(1))

    def remote(src, dst, sems, k):
        copy = pltpu.make_async_remote_copy(
            src_ref=src,
            dst_ref=dst,
            send_sem=sems.at[0, k],
            recv_sem=sems.at[1, inverse(k)],
            device_id=peer(k),
            device_id_type=MESH,
        )
        copy.start()
        return copy

    steps = [dy * 4 + dx * 2 for dy, dx in ORDER]
    pairs = [k for first in steps for k in (first, first + 1) if k]
    m_copy = {k: remote(msg.at[k], got.at[inverse(k)], msem, k) for k in pairs}
    q_copy = {k: remote(qry, qall.at[inverse(k)], qsem, k) for k in pairs}

    flat = jnp.where(lane16 < 64, rel * 128.0 + slot, rel * 16.0 + slot)
    eye = row128 == col128
    for r in range(16):
        column = jnp.sum(jnp.where(eye[:64], flat[r : r + 1, :], 0.0), 1, keepdims=True)
        flatcol[r * 64 : (r + 1) * 64, :] = jnp.broadcast_to(column, (64, 128))

    load.wait()
    r_copy = {}
    lanes = lax.broadcasted_iota(jnp.int32, (128, 2048), 1).astype(f32)
    for number, first in enumerate(steps):
        for k in (first, first + 1):
            if k:
                m_copy[inverse(k)].wait_recv()
            column = jnp.sum(jnp.where(eye, got[k, 0:1, 0:128], 0.0), 1, keepdims=True)
            hot[(k % 2) * 128 : (k % 2 + 1) * 128, :] = jnp.where(column == lanes, 1.0, 0.0).astype(bf16)

        def gather(n, carry, first=first):
            cols = pl.ds(pl.multiple_of(n * 256, 256), 256)
            rows = jnp.dot(hot[...], psg[:, cols], preferred_element_type=f32).astype(bf16)
            if first:
                reply[first, :, cols] = rows[:128]
            else:
                back[0, :, cols] = rows[:128]
            reply[first + 1, :, cols] = rows[128:]
            return carry

        lax.fori_loop(0, 4, gather, 0)
        for k in (first, first + 1):
            if k:
                r_copy[k] = remote(reply.at[k], back.at[inverse(k)], rsem, k)
        if number == 3:
            relay(0, 0)
        elif number == 5:
            relay(1, 0)

    relay(2, 0)
    relay(0, 1)
    eye8 = eye[:8]
    for k in range(16):
        column = jnp.sum(jnp.where(eye8, got[k, 0:1, 128:256], 0.0), 1, keepdims=True)
        codes[k * 8 : (k + 1) * 8, :] = jnp.broadcast_to(column, (8, 128))
    for k in pairs:
        q_copy[k].wait_recv()
    code = codes[...].astype(jnp.int32) - 1
    slot_row = lax.broadcasted_iota(jnp.int32, (128, 256), 0)
    slot_col = lax.broadcasted_iota(jnp.int32, (128, 256), 1)
    code2 = jnp.concatenate([code, code], 1)
    pick = (slot_col == (slot_row // 8) * 16 + (code2 >> 2)) & (code2 >= 0)
    chosen = jnp.where(pick, 1.0, 0.0).astype(bf16)
    queries_all = qall[...].reshape(256, D)
    frows[...] = jnp.dot(chosen, queries_all, preferred_element_type=f32).astype(bf16)
    cluster = code[:, 0:1] & 3

    def score_step(n, carry):
        rows = pl.ds(pl.multiple_of(n * 512, 512), 512)
        s = lax.dot_general(frows[...], psg[rows, :], NT, preferred_element_type=f32)
        score[:, rows] = jnp.where(cluster == n, s * (D ** (-0.5)), -1e30)
        return carry

    lax.fori_loop(0, 4, score_step, 0)
    relay(3, 0)
    relay(1, 1)
    peak = jnp.max(score[...], 1, keepdims=True)
    expo = jnp.exp(score[...] - peak)
    weights = (expo / jnp.sum(expo, 1, keepdims=True)).astype(bf16)
    pooled = jnp.dot(weights, psg[...], preferred_element_type=f32)
    for k in range(16):
        rows = jnp.concatenate([pooled[k * 8 : (k + 1) * 8], jnp.zeros((8, D), f32)], 0).astype(bf16)
        if k:
            pool[k] = rows
        else:
            prow[0] = rows
    p_copy = {k: remote(pool.at[k], prow.at[inverse(k)], osem, k) for k in pairs}

    def assemble(dy, fresh):
        for k in range(dy * 4, dy * 4 + 4):
            if k:
                r_copy[inverse(k)].wait_recv()
        wide = (lax.broadcasted_iota(jnp.int32, (256, 512), 1) + dy * 512).astype(f32)

        def part(n, carry):
            rows = pl.ds(pl.multiple_of(n * 256, 256), 256)
            place = jnp.concatenate([flatcol[rows, :]] * 4, 1)
            mark = jnp.where(place == wide, 1.0, 0.0).astype(bf16)
            values = back[dy * 4 : dy * 4 + 4].reshape(512, D)
            found = jnp.dot(mark, values, preferred_element_type=f32).astype(bf16)
            tok[rows, :] = found if fresh else tok[rows, :] + found
            return carry

        lax.fori_loop(0, 4, part, 0)

    relay(2, 1)
    relay(0, 2)
    relay(4, 0)
    relay(1, 2)
    relay(3, 1)
    relay(2, 2)
    assemble(0, True)
    relay(3, 2)
    relay(5, 0)
    relay(4, 1)
    assemble(2, False)
    relay(4, 2)
    relay(5, 1)
    for k in pairs:
        p_copy[k].wait_recv()
    wide = lax.broadcasted_iota(jnp.int32, (16, 256), 1).astype(f32)
    mix = jnp.zeros((16, 256), f32)
    for j in range(4):
        mix = mix + jnp.where(flat[:, 64 + j : 65 + j] == wide, 1.0, 0.0)
    summed = jnp.dot(mix.astype(bf16), prow[...].reshape(256, D), preferred_element_type=f32)
    tok[N_C:, :] = (qry[...].astype(f32) + summed * 0.25).astype(bf16)
    assemble(1, False)
    assemble(3, False)
    relay(5, 2)
    for u in range(6):
        for s in range(5, 9):
            started[u, s].wait_recv()
    for copies in (m_copy, q_copy, r_copy, p_copy, started):
        for copy in copies.values():
            copy.wait_send()


def front(own, pay, qry, passages, wq, wo, wu, wd):
    vmem = pl.BlockSpec(memory_space=pltpu.VMEM)
    hbm = pl.BlockSpec(memory_space=pl.ANY)
    weights = [jax.ShapeDtypeStruct(w.shape, bf16) for w in (wq, wo, wu, wd)]
    dma = pltpu.SemaphoreType.DMA
    return pl.pallas_call(
        front_kernel,
        out_shape=[jax.ShapeDtypeStruct((N_TOK, D), bf16)] + weights,
        in_specs=[vmem, vmem, vmem] + [hbm] * 5,
        out_specs=[vmem] + [hbm] * 4,
        scratch_shapes=[
            pltpu.VMEM((PASS_DEV, D), bf16),
            pltpu.VMEM((16, 16, D), bf16),
            pltpu.VMEM((16, 8, 256), f32),
            pltpu.VMEM((16, 8, 256), f32),
            pltpu.VMEM((256, 2048), bf16),
            pltpu.VMEM((16, 128, D), bf16),
            pltpu.VMEM((16, 128, D), bf16),
            pltpu.VMEM((128, 128), f32),
            pltpu.VMEM((128, D), bf16),
            pltpu.VMEM((128, PASS_DEV), f32),
            pltpu.VMEM((16, 16, D), bf16),
            pltpu.VMEM((16, 16, D), bf16),
            pltpu.VMEM((N_C, 128), f32),
            dma(()),
            dma((2, 16)),
            dma((2, 16)),
            dma((2, 16)),
            dma((2, 16)),
            dma((6, 9)),
            dma((6, 9)),
        ],
        compiler_params=pltpu.CompilerParams(
            collective_id=0, has_side_effects=True, vmem_limit_bytes=56 * 2**20
        ),
        cost_estimate=pl.CostEstimate(flops=2**34, bytes_accessed=50 * 2**20, transcendentals=0),
        name="front",
    )(own, pay, qry, passages, wq, wo, wu, wd)


def on_device(
    queries,
    passages,
    probe_owner,
    probe_cluster,
    pair_owner,
    pair_row,
    w_qkv,
    w_out,
    w_up,
    w_down,
    gain_one,
    gain_two,
):
    blank = jnp.full((Q_DEV, 60), -1, jnp.int32)
    own = jnp.concatenate([pair_owner[:, :, 0], probe_owner, blank], 1)
    code = 1 + jnp.arange(Q_DEV, dtype=jnp.int32)[:, None] * 4 + probe_cluster
    pay = jnp.concatenate([pair_row, code, blank * 0], 1)
    wq = jnp.transpose(w_qkv, (1, 0, 2))
    tok, wq1, wo1, wu1, wd1 = front(own, pay, queries, passages, wq, w_out, w_up, w_down)
    return layer(
        tok, wq, wq1, w_out, wo1, w_up, wu1, w_down, wd1, gain_one[None, :], gain_two[None, :]
    )


def solution(mesh):
    rows = P(("index", "rep", "tp"), None)
    lists = P(("index", "rep", "tp"), None, None)
    in_specs = (
        rows,
        P("index", None),
        rows,
        rows,
        lists,
        rows,
        P(None, None, "tp"),
        P("tp", None),
        P(None, "tp"),
        P("tp", None),
        P(),
        P(),
    )
    return jax.shard_map(
        on_device, mesh=mesh, in_specs=in_specs, out_specs=lists, check_vma=False
    )
```

```python
import math

import jax
import jax.numpy as jnp
from jax import lax
from jax.experimental import pallas as pl
from jax.experimental.pallas import tpu as pltpu
from jax.sharding import PartitionSpec as P

NT = (((1,), (1,)), ((), ()))
MESH = pl.DeviceIdType.MESH
bf16 = jnp.bfloat16
f32 = jnp.float32
D = 1024
Q_DEV = 16
PASS_DEV = 2048
N_C = 1024
N_TOK = 1040

def gelu(x):
    ax=jnp.abs(x)
    t=1.0/(1.0+(0.3275911*math.sqrt(0.5))*ax)
    e=jnp.exp2((-0.5/math.log(2.0))*(x*x))
    p=0.5*0.254829592+t*(0.5*-0.284496736+t*(0.5*1.421413741+t*(0.5*-1.453152027+t*(0.5*1.061405429))))
    return jnp.maximum(x,0.0)-ax*(p*t*e)

def norm(v,g):
    c=v-jnp.mean(v,-1,keepdims=True)
    var=jnp.mean(c*c,-1,keepdims=True)
    return c*lax.rsqrt(var+1e-5)*g

ORDER = ((2, 1), (2, 0), (1, 1), (3, 1), (1, 0), (3, 0), (0, 1), (0, 0))
UNITS = ((0, 0), (0, 1), (0, 2), (1, 0), (2, 0), (3, 0))
ROWS = (128, 64, 128, 256)


PLAN = {
    2: ((0, 0), (1, 0)),
    3: ((0, 1), (2, 0)),
    4: ((1, 1), (3, 0)),
    5: ((0, 2), (2, 1)),
    6: ((1, 2), (3, 1)),
    7: ((2, 2), (4, 0)),
}


def inverse(k):
    return ((4 - k // 4) % 4) * 4 + k % 4


def whole_kernel(
    own,
    pay,
    qry,
    psg_in,
    wq_i,
    wo_i,
    wu_i,
    wd_i,
    g1,
    g2,
    out,
    wq,
    wo,
    wu,
    wd,
    tok,
    psg_qk,
    reply_vc,
    kl,
    vl,
    ctxl,
    acc,
    ask,
    asked,
    msg,
    got,
    hot,
    back,
    codes,
    score,
    pool,
    prow,
    flatcol,
    psem,
    qsem,
    msem,
    rsem,
    osem,
    wsend,
    wrecv,
    lsem,
    fsem,
):
    psg, qs, ks, vs, ctx = (
        psg_qk.at[:PASS_DEV],
        psg_qk.at[:N_TOK],
        psg_qk.at[N_TOK:],
        reply_vc.at[:N_TOK],
        reply_vc.at[N_TOK:],
    )
    idx = lax.axis_index("index")
    z = lax.axis_index("rep")
    t = lax.axis_index("tp")
    y, xh, c = idx // 4, (idx // 2) % 2, idx % 2

    def peer(k):
        dy, dx, dc = k // 4, (k // 2) % 2, k % 2
        return (((y + dy) % 4) * 4 + ((xh + dx) % 2) * 2 + (c + dc) % 2, z, (t + dx) % 2)

    partner = (idx, z, 1 - t)
    z_up = (idx, (z + 1) % 4, t)
    z_down = (idx, (z + 3) % 4, t)
    barrier = pltpu.get_barrier_semaphore()
    for device in [peer(k) for k in range(1, 16)] + [partner, z_up, z_down]:
        pl.semaphore_signal(barrier, inc=1, device_id=device, device_id_type=MESH)
    load = pltpu.make_async_copy(psg_in, psg, psem)
    load.start()

    owner = own[...]
    rel = (((owner >> 2) - y) & 3) * 4 + (((owner >> 1) & 1) ^ xh) * 2 + ((owner & 1) ^ c)
    rel = jnp.where(owner < 0, -1, rel).astype(f32)
    sub16 = lax.broadcasted_iota(jnp.int32, (16, 128), 0).astype(f32)
    marks = [jnp.where(rel[r : r + 1, :] == sub16, 1.0, 0.0) for r in range(16)]
    onehot = jnp.concatenate(marks, 0)
    onehot16 = onehot.astype(bf16)
    row128 = lax.broadcasted_iota(jnp.int32, (128, 128), 0)
    col128 = lax.broadcasted_iota(jnp.int32, (128, 128), 1)
    same = (row128 // 64) == (col128 // 64)
    earlier = jnp.where(same & (row128 < col128), 1.0, 0.0).astype(bf16)
    block = jnp.where(same, 1.0, 0.0).astype(bf16)
    row256 = lax.broadcasted_iota(jnp.int32, (256, 256), 0)
    col256 = lax.broadcasted_iota(jnp.int32, (256, 256), 1)
    above = jnp.where(((row256 % 16) == (col256 % 16)) & (col256 < row256 - row256 % 16), 1.0, 0.0)
    lists_before = jnp.dot(above.astype(bf16), onehot16, preferred_element_type=f32).astype(bf16)
    count = jnp.dot(onehot16, earlier, preferred_element_type=f32)
    count = count + jnp.dot(lists_before, block, preferred_element_type=f32)
    slot = jnp.sum((onehot * count).reshape(16, 16, 128), 1)

    lane16 = lax.broadcasted_iota(jnp.int32, (16, 128), 1)
    target = jnp.where(lane16 < 64, slot, slot + 128.0)
    high = (pay[...] >> 5).astype(f32)
    low = (pay[...] & 31).astype(f32)
    sub256 = lax.broadcasted_iota(jnp.int32, (256, 128), 0).astype(f32)
    pad = jnp.zeros((96, 128), f32)
    table = jnp.zeros((256, 128), f32)
    for r in range(16):
        here = jnp.where(target[r : r + 1, :] == sub256, 1.0, 0.0).astype(bf16)
        digit = jnp.concatenate([marks[r] * high[r : r + 1, :], marks[r] * low[r : r + 1, :], pad], 0)
        table = table + lax.dot_general(here, digit.astype(bf16), NT, preferred_element_type=f32)
    table = jnp.transpose(table)
    table = table[:16] * 32.0 + table[16:32]
    first_row = lax.broadcasted_iota(jnp.int32, (8, 128), 0) == 0
    for k in range(16):
        msg[k] = jnp.where(first_row, table[k : k + 1, :128], table[k : k + 1, 128:])
    got[0] = msg[0]

    wide = lax.broadcasted_iota(jnp.int32, (16, 128), 1).astype(f32)
    mix = jnp.zeros((16, 128), f32)
    for j in range(4):
        place = rel[:, 64 + j : 65 + j] * 8.0 + slot[:, 64 + j : 65 + j]
        mix = mix + jnp.where(place == wide, 1.0, 0.0)
    pick = jnp.transpose(jnp.concatenate([mix, jnp.zeros((112, 128), f32)], 0)).astype(bf16)
    padded = jnp.concatenate([qry[...], jnp.zeros((112, D), bf16)], 0)
    picked = jnp.dot(pick, padded, preferred_element_type=f32)

    def fold(rows):
        return jnp.concatenate([rows[:, :512], rows[:, 512:]], 0).astype(bf16)

    for k in range(16):
        ask[k] = fold(picked[k * 8 : (k + 1) * 8])
    asked[0] = ask[0]

    pl.semaphore_wait(barrier, 18)

    def remote(src, dst, sems, k):
        copy = pltpu.make_async_remote_copy(
            src_ref=src,
            dst_ref=dst,
            send_sem=sems.at[0, k],
            recv_sem=sems.at[1, inverse(k)],
            device_id=peer(k),
            device_id_type=MESH,
        )
        copy.start()
        return copy

    steps = [dy * 4 + dx * 2 for dy, dx in ORDER]
    pairs = [k for first in steps for k in (first, first + 1) if k]
    m_copy = {k: remote(msg.at[k], got.at[inverse(k)], msem, k) for k in pairs}
    q_copy = {k: remote(ask.at[k], asked.at[inverse(k)], qsem, k) for k in pairs}

    w_in = (wq_i, wo_i, wu_i, wd_i)
    w_out = (wq.at[1], wo.at[1], wu.at[1], wd.at[1])

    def share(refs, unit, zz, cc, half=None):
        n, j = UNITS[unit]
        rows = ROWS[n]
        start = (zz * 2 + cc) * rows
        if half is not None:
            rows = rows // 2
            start = start + half * rows
        part = pl.ds(pl.multiple_of(start, 32), rows)
        return refs[n].at[j, part, :] if n == 0 else refs[n].at[part, :]

    def push(src, dst, unit, s, device):
        copy = pltpu.make_async_remote_copy(
            src_ref=src,
            dst_ref=dst,
            send_sem=wsend.at[unit, s],
            recv_sem=wrecv.at[unit, s],
            device_id=device,
            device_id_type=MESH,
        )
        copy.start()
        return copy

    started = {}
    for u in range(6):
        started[u, 0] = push(share(w_in, u, z, c), share(w_out, u, z, c), u, 0, partner)
    own_copies = []
    for n, here in enumerate((wq, wo, wu, wd)):
        own_copies.append(pltpu.make_async_copy(w_in[n], here.at[0], lsem.at[n]))
        own_copies[n].start()

    def relay(u, stage):
        def put(s, zz, half, device):
            ref = share(w_out, u, zz, c, half)
            started[u, s] = push(ref, ref, u, s, device)

        zm, zp, zo = (z + 3) % 4, (z + 1) % 4, (z + 2) % 4
        if stage == 0:
            started[u, 0].wait_recv()
            put(1, z, None, z_up)
            put(2, z, None, z_down)
            put(5, z, None, peer(1))
        elif stage == 1:
            started[u, 1].wait_recv()
            put(3, zm, 0, z_up)
            put(6, zm, None, peer(1))
            started[u, 2].wait_recv()
            put(4, zp, 1, z_down)
            put(7, zp, None, peer(1))
        else:
            started[u, 3].wait_recv()
            started[u, 4].wait_recv()
            put(8, zo, None, peer(1))

    def landed(*units):
        for u in units:
            for s in range(5, 9):
                started[u, s].wait_recv()

    flat = rel * 128.0 + slot
    eye = row128 == col128
    for r in range(16):
        column = jnp.sum(jnp.where(eye[:64], flat[r : r + 1, :], 0.0), 1, keepdims=True)
        flatcol[r * 64 : (r + 1) * 64, :] = jnp.broadcast_to(column, (64, 128))

    def probes():
        eye8 = eye[:8]
        for k in range(16):
            column = jnp.sum(jnp.where(eye8, got[k, 1:2, :], 0.0), 1, keepdims=True)
            codes[k * 8 : (k + 1) * 8, :] = jnp.broadcast_to(column, (8, 128))
        for k in pairs:
            q_copy[k].wait_recv()
        cluster = codes[:, 0:1].astype(jnp.int32) & 3
        rows16 = asked[...].reshape(256, 512)

        def score_step(n, carry):
            rows = pl.ds(pl.multiple_of(n * 512, 512), 512)
            left = lax.dot_general(rows16, psg[rows, :512], NT, preferred_element_type=f32)
            right = lax.dot_general(rows16, psg[rows, 512:], NT, preferred_element_type=f32)
            s = left.reshape(16, 2, 8, 512)[:, 0] + right.reshape(16, 2, 8, 512)[:, 1]
            score[:, rows] = jnp.where(cluster == n, s.reshape(128, 512) * (D ** (-0.5)), -1e30)
            return carry

        lax.fori_loop(0, 4, score_step, 0)
        peak = jnp.max(score[...], 1, keepdims=True)
        expo = jnp.exp(score[...] - peak)
        weights = (expo / jnp.sum(expo, 1, keepdims=True)).astype(bf16)
        pooled = jnp.dot(weights, psg[...], preferred_element_type=f32)
        for k in range(16):
            rows = fold(pooled[k * 8 : (k + 1) * 8])
            if k:
                pool[k] = rows
            else:
                prow[0] = rows
        return {k: remote(pool.at[k], prow.at[inverse(k)], osem, k) for k in pairs}

    load.wait()
    r_copy = {}
    waited = set()
    lanes = lax.broadcasted_iota(jnp.int32, (128, 2048), 1).astype(f32)
    for number, first in enumerate(steps):
        for k in (first, first + 1):
            if k and k not in waited:
                m_copy[inverse(k)].wait_recv()
                waited.add(k)
            column = jnp.sum(jnp.where(eye, got[k, 0:1, :], 0.0), 1, keepdims=True)
            hot[(k % 2) * 128 : (k % 2 + 1) * 128, :] = jnp.where(column == lanes, 1.0, 0.0).astype(bf16)

        def gather(n, carry, first=first):
            cols = pl.ds(pl.multiple_of(n * 256, 256), 256)
            rows = jnp.dot(hot[...], psg[:, cols], preferred_element_type=f32).astype(bf16)
            if first:
                reply_vc[first * 128 : (first + 1) * 128, cols] = rows[:128]
            else:
                back[0, :, cols] = rows[:128]
            reply_vc[(first + 1) * 128 : (first + 2) * 128, cols] = rows[128:]
            return carry

        lax.fori_loop(0, 4, gather, 0)
        for k in (first, first + 1):
            if k:
                r_copy[k] = remote(reply_vc.at[k * 128 : (k + 1) * 128], back.at[inverse(k)], rsem, k)
        if number == 2:
            for k in pairs:
                if k not in waited:
                    m_copy[inverse(k)].wait_recv()
                    waited.add(k)
            p_copy = probes()
        for u, stage in PLAN.get(number, ()):
            relay(u, stage)

    def assemble(dy, fresh):
        for k in range(dy * 4, dy * 4 + 4):
            if k:
                r_copy[inverse(k)].wait_recv()
        wide = (lax.broadcasted_iota(jnp.int32, (256, 512), 1) + dy * 512).astype(f32)

        def part(n, carry):
            rows = pl.ds(pl.multiple_of(n * 256, 256), 256)
            place = jnp.concatenate([flatcol[rows, :]] * 4, 1)
            mark = jnp.where(place == wide, 1.0, 0.0).astype(bf16)
            values = back[dy * 4 : dy * 4 + 4].reshape(512, D)
            found = jnp.dot(mark, values, preferred_element_type=f32).astype(bf16)
            tok[rows, :] = found if fresh else tok[rows, :] + found
            return carry

        lax.fori_loop(0, 4, part, 0)

    relay(3, 2)
    assemble(0, True)
    relay(4, 1)
    assemble(2, False)
    relay(5, 0)
    for k in pairs:
        p_copy[k].wait_recv()
    wide = lax.broadcasted_iota(jnp.int32, (16, 256), 1).astype(f32)
    halves = []
    for half in range(2):
        mix = jnp.zeros((16, 256), f32)
        for j in range(4):
            place = rel[:, 64 + j : 65 + j] * 16.0 + slot[:, 64 + j : 65 + j] + half * 8.0
            mix = mix + jnp.where(place == wide, 1.0, 0.0)
        halves.append(
            jnp.dot(mix.astype(bf16), prow[...].reshape(256, 512), preferred_element_type=f32)
        )
    summed = jnp.concatenate(halves, 1)
    tok[N_C:, :] = (qry[...].astype(f32) + summed * 0.25).astype(bf16)
    assemble(1, False)
    assemble(3, False)
    for copy in r_copy.values():
        copy.wait_send()

    for i in range(2):
        if i == 0:
            own_copies[0].wait()
        else:
            landed(0, 1, 2)
        def qkv_step(n,carry):
            col=pl.ds(pl.multiple_of(n*256,256),256)
            ocol=pl.ds(pl.multiple_of(i*512+n*256,256),256)
            for j,ref in enumerate((qs,ks,vs)):
                r=jnp.dot(tok[...],wq[i,j,:,col],preferred_element_type=f32)
                if j==0: r=r*0.125
                ref[:,ocol]=r.astype(bf16)
            return carry
        lax.fori_loop(0,2,qkv_step,0)
    relay(4, 2)
    relay(5, 1)
    kl[...]=ks[N_C:,:].astype(f32); vl[...]=vs[N_C:,:].astype(f32)
    ctxl[...]=jnp.zeros_like(ctxl)
    lane=lax.broadcasted_iota(jnp.int32,(64,256),1)//64
    ones_bd=(lax.broadcasted_iota(jnp.int32,(256,256),0)//64==lax.broadcasted_iota(jnp.int32,(256,256),1)//64).astype(bf16)
    low=lax.broadcasted_iota(jnp.int32,(80,128),1)<64
    rowid=lax.broadcasted_iota(jnp.int32,(16,256),0)
    def bd(x):
        return jnp.concatenate([jnp.where(lane==h,x,jnp.zeros_like(x)) for h in range(4)],0)
    def att(g,carry):
        rows=pl.ds(pl.multiple_of(g*64,64),64)
        es=[];els=[];
        for j in range(4):
            cs=slice(j*256,(j+1)*256)
            Q=jnp.concatenate([qs[rows,cs],qs[N_C:,cs]],0)
            klb=jnp.broadcast_to(kl[pl.ds(g,1),cs],(64,256)).astype(bf16)
            S=lax.dot_general(Q,bd(ks[rows,cs]),NT,preferred_element_type=f32)
            SL=lax.dot_general(Q,bd(klb),NT,preferred_element_type=f32)
            ms=[]
            for b in range(2):
                X=S[:,b*128:(b+1)*128]
                mA=jnp.max(jnp.where(low,X,-jnp.inf),1,keepdims=True)
                mB=jnp.max(jnp.where(low,-jnp.inf,X),1,keepdims=True)
                ms.append(jnp.where(low,mA,mB))
            m=jnp.maximum(jnp.concatenate(ms,1),SL)
            es.append(jnp.exp(S-m).astype(bf16)); els.append(jnp.exp(SL-m))
        den=jnp.dot(jnp.concatenate(es,0),ones_bd,preferred_element_type=f32)
        for j in range(4):
            cs=slice(j*256,(j+1)*256)
            pv=jnp.dot(es[j],bd(vs[rows,cs]),preferred_element_type=f32)
            c=(pv+els[j]*vl[pl.ds(g,1),cs])/(den[j*80:(j+1)*80]+els[j])
            ctx[rows,cs]=c[:64].astype(bf16)
            ctxl[:,cs]+=jnp.where(rowid==g,c[64:],0.0)
        return carry
    lax.fori_loop(0,16,att,0)
    ctx[N_C:,:]=ctxl[...].astype(bf16)
    relay(5, 2)
    own_copies[1].wait()
    landed(3)
    def outp(rows,n):
        a=jnp.dot(ctx[rows,:512],wo[0],preferred_element_type=f32)+jnp.dot(ctx[rows,512:],wo[1],preferred_element_type=f32)
        return norm(tok[rows,:].astype(f32)+a,g1[...]).astype(bf16).astype(f32)
    def put(g,y):
        for c in range(8): acc[c,pl.ds(16+g,64,stride=16),:]=y[:,c*128:(c+1)*128]
    def outc(i,carry):
        h=outp(pl.ds(pl.multiple_of(i*256,256),256),256)
        for l in range(4):
            put(i*4+l,h[l*64:(l+1)*64])
        return carry
    lax.fori_loop(0,3,outc,0)
    h=outp(slice(768,1040),272)
    for l in range(4):
        put(12+l,h[l*64:(l+1)*64])
    for c in range(8): acc[c,0:16,:]=h[256:,c*128:(c+1)*128]
    own_copies[2].wait()
    own_copies[3].wait()
    landed(4, 5)
    def ffn(r,carry):
        rows=pl.ds(pl.multiple_of(r*208,16),208)
        t=jnp.concatenate([acc[c,rows,:] for c in range(8)],1)
        x=t.astype(bf16)
        acts=[]
        for i in range(2):
            for n in range(4):
                u=jnp.dot(x,wu[i,:,n*512:(n+1)*512],preferred_element_type=f32)
                acts.append(gelu(u).astype(bf16))
        for i in range(2):
            t=t+jnp.dot(jnp.concatenate(acts[i*4:(i+1)*4],1),wd[i],preferred_element_type=f32)
        tok[rows,:]=norm(t,g2[...]).astype(bf16)
        pltpu.make_async_copy(tok.at[rows],out.at[rows],fsem.at[r]).start()
        return carry
    lax.fori_loop(0,5,ffn,0)
    for r in range(5):
        rows=slice(r*208,(r+1)*208)
        pltpu.make_async_copy(tok.at[rows],out.at[rows],fsem.at[r]).wait()
    for copies in (m_copy, q_copy, p_copy, started):
        for copy in copies.values():
            copy.wait_send()


def whole(own, pay, qry, passages, wq, wo, wu, wd, g1, g2):
    vmem = pl.BlockSpec(memory_space=pltpu.VMEM)
    hbm = pl.BlockSpec(memory_space=pl.ANY)
    dma = pltpu.SemaphoreType.DMA
    return pl.pallas_call(
        whole_kernel,
        out_shape=jax.ShapeDtypeStruct((N_TOK, D), bf16),
        in_specs=[vmem, vmem, vmem] + [hbm] * 5 + [vmem, vmem],
        out_specs=hbm,
        scratch_shapes=[
            pltpu.VMEM((2, 3, D, 512), bf16),
            pltpu.VMEM((2, 512, D), bf16),
            pltpu.VMEM((2, D, 2048), bf16),
            pltpu.VMEM((2, 2048, D), bf16),
            pltpu.VMEM((N_TOK, D), bf16),
            pltpu.VMEM((2 * N_TOK, D), bf16),
            pltpu.VMEM((2 * N_TOK, D), bf16),
            pltpu.VMEM((16, D), f32),
            pltpu.VMEM((16, D), f32),
            pltpu.VMEM((16, D), f32),
            pltpu.VMEM((8, N_TOK, 128), f32),
            pltpu.VMEM((16, 16, 512), bf16),
            pltpu.VMEM((16, 16, 512), bf16),
            pltpu.VMEM((16, 8, 128), f32),
            pltpu.VMEM((16, 8, 128), f32),
            pltpu.VMEM((256, 2048), bf16),
            pltpu.VMEM((16, 128, D), bf16),
            pltpu.VMEM((128, 128), f32),
            pltpu.VMEM((128, PASS_DEV), f32),
            pltpu.VMEM((16, 16, 512), bf16),
            pltpu.VMEM((16, 16, 512), bf16),
            pltpu.VMEM((N_C, 128), f32),
            dma(()),
            dma((2, 16)),
            dma((2, 16)),
            dma((2, 16)),
            dma((2, 16)),
            dma((6, 9)),
            dma((6, 9)),
            dma((4,)),
            dma((5,)),
        ],
        compiler_params=pltpu.CompilerParams(
            collective_id=0, has_side_effects=True, vmem_limit_bytes=62 * 2**20
        ),
        cost_estimate=pl.CostEstimate(flops=2**35, bytes_accessed=50 * 2**20, transcendentals=0),
        name="whole",
    )(own, pay, qry, passages, wq, wo, wu, wd, g1, g2)


def on_device(
    queries,
    passages,
    probe_owner,
    probe_cluster,
    pair_owner,
    pair_row,
    w_qkv,
    w_out,
    w_up,
    w_down,
    gain_one,
    gain_two,
):
    blank = jnp.full((Q_DEV, 60), -1, jnp.int32)
    own = jnp.concatenate([pair_owner[:, :, 0], probe_owner, blank], 1)
    pay = jnp.concatenate([pair_row, probe_cluster, blank * 0], 1)
    wq = jnp.transpose(w_qkv, (1, 0, 2))
    rows = whole(
        own, pay, queries, passages, wq, w_out, w_up, w_down, gain_one[None, :], gain_two[None, :]
    )
    return jnp.transpose(rows.reshape(65, 16, D), (1, 0, 2))


def solution(mesh):
    rows = P(("index", "rep", "tp"), None)
    lists = P(("index", "rep", "tp"), None, None)
    in_specs = (
        rows,
        P("index", None),
        rows,
        rows,
        lists,
        rows,
        P(None, None, "tp"),
        P("tp", None),
        P(None, "tp"),
        P("tp", None),
        P(),
        P(),
    )
    return jax.shard_map(
        on_device, mesh=mesh, in_specs=in_specs, out_specs=lists, check_vma=False
    )
```

```python
import math

import jax
import jax.numpy as jnp
from jax import lax
from jax.experimental import pallas as pl
from jax.experimental.pallas import tpu as pltpu
from jax.sharding import PartitionSpec as P

NT = (((1,), (1,)), ((), ()))
MESH = pl.DeviceIdType.MESH
bf16 = jnp.bfloat16
f32 = jnp.float32
D = 1024
Q_DEV = 16
PASS_DEV = 2048
N_C = 1024
N_TOK = 1040

def gelu(x):
    ax=jnp.abs(x)
    t=1.0/(1.0+(0.3275911*math.sqrt(0.5))*ax)
    e=jnp.exp2((-0.5/math.log(2.0))*(x*x))
    p=0.5*0.254829592+t*(0.5*-0.284496736+t*(0.5*1.421413741+t*(0.5*-1.453152027+t*(0.5*1.061405429))))
    return jnp.maximum(x,0.0)-ax*(p*t*e)

def norm(v,g):
    c=v-jnp.mean(v,-1,keepdims=True)
    var=jnp.mean(c*c,-1,keepdims=True)
    return c*lax.rsqrt(var+1e-5)*g

ORDER = ((2, 1), (2, 0), (1, 1), (3, 1), (1, 0), (3, 0), (0, 1), (0, 0))
UNITS = ((0, 0), (0, 1), (0, 2), (1, 0), (2, 0), (3, 0))
ROWS = (128, 64, 128, 256)


PLAN = {
    2: ((0, 0), (1, 0)),
    3: ((0, 1), (2, 0)),
    4: ((1, 1), (3, 0)),
    5: ((0, 2), (2, 1)),
    6: ((1, 2), (3, 1)),
    7: ((2, 2), (4, 0)),
}


def inverse(k):
    return ((4 - k // 4) % 4) * 4 + k % 4


def whole_kernel(
    own,
    pay,
    qry,
    psg_in,
    wq_i,
    wo_i,
    wu_i,
    wd_i,
    g1,
    g2,
    out,
    wq,
    wo,
    wu,
    wd,
    tok,
    psg_qk,
    reply_vc,
    sl,
    vl,
    ctxl,
    acc,
    ask,
    asked,
    msg,
    got,
    hot,
    back,
    codes,
    score,
    pool,
    prow,
    flatcol,
    psem,
    qsem,
    msem,
    rsem,
    osem,
    wsend,
    wrecv,
    lsem,
    fsem,
):
    psg, qs, ks, vs, ctx = (
        psg_qk.at[:PASS_DEV],
        psg_qk.at[:N_TOK],
        psg_qk.at[N_TOK:],
        reply_vc.at[:N_TOK],
        reply_vc.at[N_TOK:],
    )
    idx = lax.axis_index("index")
    z = lax.axis_index("rep")
    t = lax.axis_index("tp")
    y, xh, c = idx // 4, (idx // 2) % 2, idx % 2

    def peer(k):
        dy, dx, dc = k // 4, (k // 2) % 2, k % 2
        return (((y + dy) % 4) * 4 + ((xh + dx) % 2) * 2 + (c + dc) % 2, z, (t + dx) % 2)

    partner = (idx, z, 1 - t)
    z_up = (idx, (z + 1) % 4, t)
    z_down = (idx, (z + 3) % 4, t)
    z_across = (idx, (z + 2) % 4, t)
    barrier = pltpu.get_barrier_semaphore()
    for device in [peer(k) for k in range(1, 16)] + [partner, z_up, z_down, z_across]:
        pl.semaphore_signal(barrier, inc=1, device_id=device, device_id_type=MESH)
    load = pltpu.make_async_copy(psg_in, psg, psem)
    load.start()

    owner = own[...]
    rel = (((owner >> 2) - y) & 3) * 4 + (((owner >> 1) & 1) ^ xh) * 2 + ((owner & 1) ^ c)
    rel = jnp.where(owner < 0, -1, rel).astype(f32)
    sub16 = lax.broadcasted_iota(jnp.int32, (16, 128), 0).astype(f32)
    marks = [jnp.where(rel[r : r + 1, :] == sub16, 1.0, 0.0) for r in range(16)]
    onehot = jnp.concatenate(marks, 0)
    onehot16 = onehot.astype(bf16)
    row128 = lax.broadcasted_iota(jnp.int32, (128, 128), 0)
    col128 = lax.broadcasted_iota(jnp.int32, (128, 128), 1)
    same = (row128 // 64) == (col128 // 64)
    earlier = jnp.where(same & (row128 < col128), 1.0, 0.0).astype(bf16)
    block = jnp.where(same, 1.0, 0.0).astype(bf16)
    row256 = lax.broadcasted_iota(jnp.int32, (256, 256), 0)
    col256 = lax.broadcasted_iota(jnp.int32, (256, 256), 1)
    above = jnp.where(((row256 % 16) == (col256 % 16)) & (col256 < row256 - row256 % 16), 1.0, 0.0)
    lists_before = jnp.dot(above.astype(bf16), onehot16, preferred_element_type=f32).astype(bf16)
    count = jnp.dot(onehot16, earlier, preferred_element_type=f32)
    count = count + jnp.dot(lists_before, block, preferred_element_type=f32)
    slot = jnp.sum((onehot * count).reshape(16, 16, 128), 1)

    lane16 = lax.broadcasted_iota(jnp.int32, (16, 128), 1)
    target = jnp.where(lane16 < 64, slot, slot + 128.0)
    high = (pay[...] >> 5).astype(f32)
    low = (pay[...] & 31).astype(f32)
    sub256 = lax.broadcasted_iota(jnp.int32, (256, 128), 0).astype(f32)
    pad = jnp.zeros((96, 128), f32)
    table = jnp.zeros((256, 128), f32)
    for r in range(16):
        here = jnp.where(target[r : r + 1, :] == sub256, 1.0, 0.0).astype(bf16)
        digit = jnp.concatenate([marks[r] * high[r : r + 1, :], marks[r] * low[r : r + 1, :], pad], 0)
        table = table + lax.dot_general(here, digit.astype(bf16), NT, preferred_element_type=f32)
    table = jnp.transpose(table)
    table = table[:16] * 32.0 + table[16:32]
    first_row = lax.broadcasted_iota(jnp.int32, (8, 128), 0) == 0
    for k in range(16):
        msg[k] = jnp.where(first_row, table[k : k + 1, :128], table[k : k + 1, 128:])
    got[0] = msg[0]

    wide = lax.broadcasted_iota(jnp.int32, (16, 128), 1).astype(f32)
    mix = jnp.zeros((16, 128), f32)
    for j in range(4):
        place = rel[:, 64 + j : 65 + j] * 8.0 + slot[:, 64 + j : 65 + j]
        mix = mix + jnp.where(place == wide, 1.0, 0.0)
    pick = jnp.transpose(jnp.concatenate([mix, jnp.zeros((112, 128), f32)], 0)).astype(bf16)
    padded = jnp.concatenate([qry[...], jnp.zeros((112, D), bf16)], 0)
    picked = jnp.dot(pick, padded, preferred_element_type=f32)

    def fold(rows):
        return jnp.concatenate([rows[:, :512], rows[:, 512:]], 0).astype(bf16)

    for k in range(16):
        ask[k] = fold(picked[k * 8 : (k + 1) * 8])
    asked[0] = ask[0]

    pl.semaphore_wait(barrier, 19)

    def remote(src, dst, sems, k):
        copy = pltpu.make_async_remote_copy(
            src_ref=src,
            dst_ref=dst,
            send_sem=sems.at[0, k],
            recv_sem=sems.at[1, inverse(k)],
            device_id=peer(k),
            device_id_type=MESH,
        )
        copy.start()
        return copy

    steps = [dy * 4 + dx * 2 for dy, dx in ORDER]
    pairs = [k for first in steps for k in (first, first + 1) if k]
    m_copy = {k: remote(msg.at[k], got.at[inverse(k)], msem, k) for k in pairs}
    q_copy = {k: remote(ask.at[k], asked.at[inverse(k)], qsem, k) for k in pairs}

    w_in = (wq_i, wo_i, wu_i, wd_i)
    w_out = (wq.at[1], wo.at[1], wu.at[1], wd.at[1])

    def share(refs, unit, zz, cc, half=None):
        n, j = UNITS[unit]
        rows = ROWS[n]
        start = (zz * 2 + cc) * rows
        if half is not None:
            rows = rows // 2
            start = start + half * rows
        part = pl.ds(pl.multiple_of(start, 32), rows)
        return refs[n].at[j, part, :] if n == 0 else refs[n].at[part, :]

    def push(src, dst, unit, s, device):
        copy = pltpu.make_async_remote_copy(
            src_ref=src,
            dst_ref=dst,
            send_sem=wsend.at[unit, s],
            recv_sem=wrecv.at[unit, s],
            device_id=device,
            device_id_type=MESH,
        )
        copy.start()
        return copy

    started = {}
    for u in range(6):
        started[u, 0] = push(share(w_in, u, z, c), share(w_out, u, z, c), u, 0, partner)
    own_copies = []
    for n, here in enumerate((wq, wo, wu, wd)):
        own_copies.append(pltpu.make_async_copy(w_in[n], here.at[0], lsem.at[n]))
        own_copies[n].start()

    def relay(u, stage):
        def put(s, zz, half, device):
            ref = share(w_out, u, zz, c, half)
            started[u, s] = push(ref, ref, u, s, device)

        zm, zp, zo = (z + 3) % 4, (z + 1) % 4, (z + 2) % 4
        if stage == 0:
            started[u, 0].wait_recv()
            put(1, z, None, z_up)
            put(2, z, None, z_down)
            if u >= 4:
                put(3, z, None, z_across)
            put(5, z, None, peer(1))
        elif u >= 4:
            for s, zz in ((1, zm), (2, zp), (3, zo)):
                started[u, s].wait_recv()
                put(s + 5, zz, None, peer(1))
        elif stage == 1:
            started[u, 1].wait_recv()
            put(3, zm, 0, z_up)
            put(6, zm, None, peer(1))
            started[u, 2].wait_recv()
            put(4, zp, 1, z_down)
            put(7, zp, None, peer(1))
        else:
            started[u, 3].wait_recv()
            started[u, 4].wait_recv()
            put(8, zo, None, peer(1))

    def landed(*units):
        for u in units:
            for s in range(5, 9):
                started[u, s].wait_recv()

    flat = rel * 128.0 + slot
    eye = row128 == col128
    for r in range(16):
        column = jnp.sum(jnp.where(eye[:64], flat[r : r + 1, :], 0.0), 1, keepdims=True)
        flatcol[r * 64 : (r + 1) * 64, :] = jnp.broadcast_to(column, (64, 128))

    def probes():
        eye8 = eye[:8]
        for k in range(16):
            column = jnp.sum(jnp.where(eye8, got[k, 1:2, :], 0.0), 1, keepdims=True)
            codes[k * 8 : (k + 1) * 8, :] = jnp.broadcast_to(column, (8, 128))
        for k in pairs:
            q_copy[k].wait_recv()
        cluster = codes[:, 0:1].astype(jnp.int32) & 3
        rows16 = asked[...].reshape(256, 512)

        def score_step(n, carry):
            rows = pl.ds(pl.multiple_of(n * 512, 512), 512)
            left = lax.dot_general(rows16, psg[rows, :512], NT, preferred_element_type=f32)
            right = lax.dot_general(rows16, psg[rows, 512:], NT, preferred_element_type=f32)
            s = left.reshape(16, 2, 8, 512)[:, 0] + right.reshape(16, 2, 8, 512)[:, 1]
            score[:, rows] = jnp.where(cluster == n, s.reshape(128, 512) * (D ** (-0.5)), -1e30)
            return carry

        lax.fori_loop(0, 4, score_step, 0)
        peak = jnp.max(score[...], 1, keepdims=True)
        expo = jnp.exp(score[...] - peak)
        weights = (expo / jnp.sum(expo, 1, keepdims=True)).astype(bf16)
        pooled = jnp.dot(weights, psg[...], preferred_element_type=f32)
        for k in range(16):
            rows = fold(pooled[k * 8 : (k + 1) * 8])
            if k:
                pool[k] = rows
            else:
                prow[0] = rows
        return {k: remote(pool.at[k], prow.at[inverse(k)], osem, k) for k in pairs}

    load.wait()
    r_copy = {}
    waited = set()
    lanes = lax.broadcasted_iota(jnp.int32, (128, 2048), 1).astype(f32)
    for number, first in enumerate(steps):
        for k in (first, first + 1):
            if k and k not in waited:
                m_copy[inverse(k)].wait_recv()
                waited.add(k)
            column = jnp.sum(jnp.where(eye, got[k, 0:1, :], 0.0), 1, keepdims=True)
            hot[(k % 2) * 128 : (k % 2 + 1) * 128, :] = jnp.where(column == lanes, 1.0, 0.0).astype(bf16)

        def gather(n, carry, first=first):
            cols = pl.ds(pl.multiple_of(n * 256, 256), 256)
            rows = jnp.dot(hot[...], psg[:, cols], preferred_element_type=f32).astype(bf16)
            if first:
                reply_vc[first * 128 : (first + 1) * 128, cols] = rows[:128]
            else:
                back[0, :, cols] = rows[:128]
            reply_vc[(first + 1) * 128 : (first + 2) * 128, cols] = rows[128:]
            return carry

        lax.fori_loop(0, 4, gather, 0)
        for k in (first, first + 1):
            if k:
                r_copy[k] = remote(reply_vc.at[k * 128 : (k + 1) * 128], back.at[inverse(k)], rsem, k)
        if number == 2:
            for k in pairs:
                if k not in waited:
                    m_copy[inverse(k)].wait_recv()
                    waited.add(k)
            p_copy = probes()
        for u, stage in PLAN.get(number, ()):
            relay(u, stage)

    def assemble(dy, fresh):
        for k in range(dy * 4, dy * 4 + 4):
            if k:
                r_copy[inverse(k)].wait_recv()
        wide = (lax.broadcasted_iota(jnp.int32, (256, 512), 1) + dy * 512).astype(f32)

        def part(n, carry):
            rows = pl.ds(pl.multiple_of(n * 256, 256), 256)
            place = jnp.concatenate([flatcol[rows, :]] * 4, 1)
            mark = jnp.where(place == wide, 1.0, 0.0).astype(bf16)
            values = back[dy * 4 : dy * 4 + 4].reshape(512, D)
            found = jnp.dot(mark, values, preferred_element_type=f32).astype(bf16)
            tok[rows, :] = found if fresh else tok[rows, :] + found
            return carry

        lax.fori_loop(0, 4, part, 0)

    relay(3, 2)
    assemble(0, True)
    assemble(2, False)
    relay(5, 0)
    for k in pairs:
        p_copy[k].wait_recv()
    wide = lax.broadcasted_iota(jnp.int32, (16, 256), 1).astype(f32)
    halves = []
    for half in range(2):
        mix = jnp.zeros((16, 256), f32)
        for j in range(4):
            place = rel[:, 64 + j : 65 + j] * 16.0 + slot[:, 64 + j : 65 + j] + half * 8.0
            mix = mix + jnp.where(place == wide, 1.0, 0.0)
        halves.append(
            jnp.dot(mix.astype(bf16), prow[...].reshape(256, 512), preferred_element_type=f32)
        )
    summed = jnp.concatenate(halves, 1)
    tok[N_C:, :] = (qry[...].astype(f32) + summed * 0.25).astype(bf16)
    assemble(1, False)
    assemble(3, False)
    for copy in r_copy.values():
        copy.wait_send()

    for i in range(2):
        if i == 0:
            own_copies[0].wait()
        else:
            landed(0, 1, 2)
        def qkv_step(n,carry):
            col=pl.ds(pl.multiple_of(n*256,256),256)
            ocol=pl.ds(pl.multiple_of(i*512+n*256,256),256)
            for j,ref in enumerate((qs,ks,vs)):
                r=jnp.dot(tok[...],wq[i,j,:,col],preferred_element_type=f32)
                if j==0: r=r*0.125
                ref[:,ocol]=r.astype(bf16)
            return carry
        lax.fori_loop(0,2,qkv_step,0)
    relay(4, 2)
    vl[...]=vs[N_C:,:].astype(f32)
    ctxl[...]=jnp.zeros_like(ctxl)
    lane=lax.broadcasted_iota(jnp.int32,(64,256),1)//64
    ones_bd=(lax.broadcasted_iota(jnp.int32,(256,256),0)//64==lax.broadcasted_iota(jnp.int32,(256,256),1)//64).astype(bf16)
    bd_mask=lax.broadcasted_iota(jnp.int32,(256,256),0)//64==lax.broadcasted_iota(jnp.int32,(256,256),1)//64
    low=lax.broadcasted_iota(jnp.int32,(80,128),1)<64
    rowid=lax.broadcasted_iota(jnp.int32,(16,256),0)
    def bd(x):
        return jnp.concatenate([jnp.where(lane==h,x,jnp.zeros_like(x)) for h in range(4)],0)
    lead_mask=lax.broadcasted_iota(jnp.int32,(16,256),1)//64
    for j in range(4):
        cs=slice(j*256,(j+1)*256)
        kj=ks[N_C:,cs]
        rows_hl=jnp.concatenate([jnp.where(lead_mask==h,kj,jnp.zeros_like(kj)) for h in range(4)]+[jnp.zeros((64,256),bf16)],0)
        sl[:,j*128:(j+1)*128]=lax.dot_general(qs[:,cs],rows_hl,NT,preferred_element_type=f32)
    erow=lax.broadcasted_iota(jnp.int32,(256,256),0)%128
    ecol=lax.broadcasted_iota(jnp.int32,(256,256),1)
    def att(g,carry):
        rows=pl.ds(pl.multiple_of(g*64,64),64)
        expand=jnp.where(erow==(ecol//64)*16+g,1.0,0.0).astype(bf16)
        parts=[]
        for j in range(4):
            x=jnp.concatenate([sl[rows,j*128:(j+1)*128],sl[N_C:,j*128:(j+1)*128]],0)
            hi=x.astype(bf16)
            parts.append(jnp.concatenate([hi,(x-hi.astype(f32)).astype(bf16)],1))
        SLall=jnp.dot(jnp.concatenate(parts,0),expand,preferred_element_type=f32)
        es=[];els=[]
        for j in range(4):
            cs=slice(j*256,(j+1)*256)
            Q=jnp.concatenate([qs[rows,cs],qs[N_C:,cs]],0)
            kt=jnp.transpose(jnp.concatenate([ks[rows,cs],ks[rows,cs]],0))
            kt=jnp.concatenate([kt,kt],1)
            S=jnp.dot(Q,jnp.where(bd_mask,kt,jnp.zeros_like(kt)),preferred_element_type=f32)
            SL=SLall[j*80:(j+1)*80]
            ms=[]
            for b in range(2):
                X=S[:,b*128:(b+1)*128]
                mA=jnp.max(jnp.where(low,X,-jnp.inf),1,keepdims=True)
                mB=jnp.max(jnp.where(low,-jnp.inf,X),1,keepdims=True)
                ms.append(jnp.where(low,mA,mB))
            m=jnp.maximum(jnp.concatenate(ms,1),SL)
            es.append(jnp.exp(S-m).astype(bf16)); els.append(jnp.exp(SL-m))
        den=jnp.dot(jnp.concatenate(es,0),ones_bd,preferred_element_type=f32)
        for j in range(4):
            cs=slice(j*256,(j+1)*256)
            pv=jnp.dot(es[j],bd(vs[rows,cs]),preferred_element_type=f32)
            c=(pv+els[j]*vl[pl.ds(g,1),cs])/(den[j*80:(j+1)*80]+els[j])
            ctx[rows,cs]=c[:64].astype(bf16)
            ctxl[:,cs]+=jnp.where(rowid==g,c[64:],0.0)
        return carry
    lax.fori_loop(0, 16, att, 0, unroll=4)
    ctx[N_C:,:]=ctxl[...].astype(bf16)
    relay(5, 2)
    own_copies[1].wait()
    landed(3)
    def outp(rows,n):
        a=jnp.dot(ctx[rows,:512],wo[0],preferred_element_type=f32)+jnp.dot(ctx[rows,512:],wo[1],preferred_element_type=f32)
        return norm(tok[rows,:].astype(f32)+a,g1[...]).astype(bf16).astype(f32)
    def put(g,y):
        for c in range(8): acc[c,pl.ds(16+g,64,stride=16),:]=y[:,c*128:(c+1)*128]
    def outc(i,carry):
        h=outp(pl.ds(pl.multiple_of(i*256,256),256),256)
        for l in range(4):
            put(i*4+l,h[l*64:(l+1)*64])
        return carry
    lax.fori_loop(0,3,outc,0)
    h=outp(slice(768,1040),272)
    for l in range(4):
        put(12+l,h[l*64:(l+1)*64])
    for c in range(8): acc[c,0:16,:]=h[256:,c*128:(c+1)*128]
    own_copies[2].wait()
    own_copies[3].wait()
    landed(4, 5)
    def ffn(r,carry):
        rows=pl.ds(pl.multiple_of(r*208,16),208)
        t=jnp.concatenate([acc[c,rows,:] for c in range(8)],1)
        x=t.astype(bf16)
        acts=[]
        for i in range(2):
            for n in range(4):
                u=jnp.dot(x,wu[i,:,n*512:(n+1)*512],preferred_element_type=f32)
                acts.append(gelu(u).astype(bf16))
        for i in range(2):
            t=t+jnp.dot(jnp.concatenate(acts[i*4:(i+1)*4],1),wd[i],preferred_element_type=f32)
        tok[rows,:]=norm(t,g2[...]).astype(bf16)
        pltpu.make_async_copy(tok.at[rows],out.at[rows],fsem.at[r]).start()
        return carry
    lax.fori_loop(0,5,ffn,0)
    for r in range(5):
        rows=slice(r*208,(r+1)*208)
        pltpu.make_async_copy(tok.at[rows],out.at[rows],fsem.at[r]).wait()
    for copies in (m_copy, q_copy, p_copy, started):
        for copy in copies.values():
            copy.wait_send()


def whole(own, pay, qry, passages, wq, wo, wu, wd, g1, g2):
    vmem = pl.BlockSpec(memory_space=pltpu.VMEM)
    hbm = pl.BlockSpec(memory_space=pl.ANY)
    dma = pltpu.SemaphoreType.DMA
    return pl.pallas_call(
        whole_kernel,
        out_shape=jax.ShapeDtypeStruct((N_TOK, D), bf16),
        in_specs=[vmem, vmem, vmem] + [hbm] * 5 + [vmem, vmem],
        out_specs=hbm,
        scratch_shapes=[
            pltpu.VMEM((2, 3, D, 512), bf16),
            pltpu.VMEM((2, 512, D), bf16),
            pltpu.VMEM((2, D, 2048), bf16),
            pltpu.VMEM((2, 2048, D), bf16),
            pltpu.VMEM((N_TOK, D), bf16),
            pltpu.VMEM((2 * N_TOK, D), bf16),
            pltpu.VMEM((2 * N_TOK, D), bf16),
            pltpu.VMEM((N_TOK, 512), f32),
            pltpu.VMEM((16, D), f32),
            pltpu.VMEM((16, D), f32),
            pltpu.VMEM((8, N_TOK, 128), f32),
            pltpu.VMEM((16, 16, 512), bf16),
            pltpu.VMEM((16, 16, 512), bf16),
            pltpu.VMEM((16, 8, 128), f32),
            pltpu.VMEM((16, 8, 128), f32),
            pltpu.VMEM((256, 2048), bf16),
            pltpu.VMEM((16, 128, D), bf16),
            pltpu.VMEM((128, 128), f32),
            pltpu.VMEM((128, PASS_DEV), f32),
            pltpu.VMEM((16, 16, 512), bf16),
            pltpu.VMEM((16, 16, 512), bf16),
            pltpu.VMEM((N_C, 128), f32),
            dma(()),
            dma((2, 16)),
            dma((2, 16)),
            dma((2, 16)),
            dma((2, 16)),
            dma((6, 9)),
            dma((6, 9)),
            dma((4,)),
            dma((5,)),
        ],
        compiler_params=pltpu.CompilerParams(
            collective_id=0, has_side_effects=True, vmem_limit_bytes=62 * 2**20
        ),
        cost_estimate=pl.CostEstimate(flops=2**35, bytes_accessed=50 * 2**20, transcendentals=0),
        name="whole",
    )(own, pay, qry, passages, wq, wo, wu, wd, g1, g2)


def on_device(
    queries,
    passages,
    probe_owner,
    probe_cluster,
    pair_owner,
    pair_row,
    w_qkv,
    w_out,
    w_up,
    w_down,
    gain_one,
    gain_two,
):
    blank = jnp.full((Q_DEV, 60), -1, jnp.int32)
    own = jnp.concatenate([pair_owner[:, :, 0], probe_owner, blank], 1)
    pay = jnp.concatenate([pair_row, probe_cluster, blank * 0], 1)
    wq = jnp.transpose(w_qkv, (1, 0, 2))
    rows = whole(
        own, pay, queries, passages, wq, w_out, w_up, w_down, gain_one[None, :], gain_two[None, :]
    )
    return jnp.transpose(rows.reshape(65, 16, D), (1, 0, 2))


def solution(mesh):
    rows = P(("index", "rep", "tp"), None)
    lists = P(("index", "rep", "tp"), None, None)
    in_specs = (
        rows,
        P("index", None),
        rows,
        rows,
        lists,
        rows,
        P(None, None, "tp"),
        P("tp", None),
        P(None, "tp"),
        P("tp", None),
        P(),
        P(),
    )
    return jax.shard_map(
        on_device, mesh=mesh, in_specs=in_specs, out_specs=lists, check_vma=False
    )
```

```python
import math

import jax
import jax.numpy as jnp
from jax import lax
from jax.experimental import pallas as pl
from jax.experimental.pallas import tpu as pltpu
from jax.sharding import PartitionSpec as P

NT = (((1,), (1,)), ((), ()))
MESH = pl.DeviceIdType.MESH
bf16 = jnp.bfloat16
f32 = jnp.float32
D = 1024
Q_DEV = 16
PASS_DEV = 2048
N_C = 1024
N_TOK = 1040

def gelu(x):
    ax=jnp.abs(x)
    t=1.0/(1.0+(0.3275911*math.sqrt(0.5))*ax)
    e=jnp.exp2((-0.5/math.log(2.0))*(x*x))
    p=0.5*0.254829592+t*(0.5*-0.284496736+t*(0.5*1.421413741+t*(0.5*-1.453152027+t*(0.5*1.061405429))))
    return jnp.maximum(x,0.0)-ax*(p*t*e)

def norm(v,g):
    c=v-jnp.mean(v,-1,keepdims=True)
    var=jnp.mean(c*c,-1,keepdims=True)
    return c*lax.rsqrt(var+1e-5)*g

ORDER = ((2, 1), (2, 0), (1, 1), (3, 1), (1, 0), (3, 0), (0, 1), (0, 0))
UNITS = ((0, 0), (0, 1), (0, 2), (1, 0), (2, 0), (3, 0))
ROWS = (128, 64, 128, 256)


PLAN = {
    2: ((0, 0), (1, 0)),
    3: ((0, 1), (2, 0)),
    4: ((1, 1), (3, 0)),
    5: ((0, 2), (2, 1)),
    6: ((1, 2), (3, 1)),
    7: ((2, 2), (4, 0)),
}


def inverse(k):
    return ((4 - k // 4) % 4) * 4 + k % 4


def whole_kernel(
    p_own,
    p_row,
    o_own,
    o_clu,
    qry,
    psg_in,
    wq_i,
    wo_i,
    wu_i,
    wd_i,
    g1,
    g2,
    out,
    wq,
    wo,
    wu,
    wd,
    tok,
    psg_qk,
    reply_vc,
    sl,
    vl,
    ctxl,
    acc,
    ask,
    asked,
    msg,
    got,
    hot,
    back,
    codes,
    score,
    pool,
    prow,
    flatcol,
    psem,
    qsem,
    msem,
    rsem,
    osem,
    wsend,
    wrecv,
    lsem,
    fsem,
    flip,
    wide_own,
    wide_row,
):
    psg, qs, ks, vs, ctx = (
        psg_qk.at[:PASS_DEV],
        psg_qk.at[:N_TOK],
        psg_qk.at[N_TOK:],
        reply_vc.at[:N_TOK],
        reply_vc.at[N_TOK:],
    )
    idx = lax.axis_index("index")
    z = lax.axis_index("rep")
    t = lax.axis_index("tp")
    y, xh, c = idx // 4, (idx // 2) % 2, idx % 2

    def peer(k):
        dy, dx, dc = k // 4, (k // 2) % 2, k % 2
        return (((y + dy) % 4) * 4 + ((xh + dx) % 2) * 2 + (c + dc) % 2, z, (t + dx) % 2)

    partner = (idx, z, 1 - t)
    z_up = (idx, (z + 1) % 4, t)
    z_down = (idx, (z + 3) % 4, t)
    z_across = (idx, (z + 2) % 4, t)
    barrier = pltpu.get_barrier_semaphore()
    for device in [peer(k) for k in range(1, 16)] + [partner, z_up, z_down, z_across]:
        pl.semaphore_signal(barrier, inc=1, device_id=device, device_id_type=MESH)
    load = pltpu.make_async_copy(psg_in, psg, psem)
    load.start()

    flip[...] = jnp.zeros_like(flip)
    flip[0, 64:68, 0:16] = o_own[...].astype(f32)
    flip[1, 64:68, 0:16] = o_clu[...].astype(f32)
    wide_own[...] = jnp.zeros_like(wide_own)
    wide_row[...] = jnp.zeros_like(wide_row)
    for r in range(16):
        wide_own[r : r + 1, 0:64] = p_own[r]
    wide_row[:, 0:64] = p_row[...]
    lane16 = lax.broadcasted_iota(jnp.int32, (16, 128), 1)
    owner = wide_own[...] + jnp.transpose(flip[0])[:16].astype(jnp.int32)
    owner = jnp.where(lane16 < 68, owner, -1)
    payload = wide_row[...] + jnp.transpose(flip[1])[:16].astype(jnp.int32)
    rel = (((owner >> 2) - y) & 3) * 4 + (((owner >> 1) & 1) ^ xh) * 2 + ((owner & 1) ^ c)
    rel = jnp.where(owner < 0, -1, rel).astype(f32)
    sub16 = lax.broadcasted_iota(jnp.int32, (16, 128), 0).astype(f32)
    marks = [jnp.where(rel[r : r + 1, :] == sub16, 1.0, 0.0) for r in range(16)]
    onehot = jnp.concatenate(marks, 0)
    onehot16 = onehot.astype(bf16)
    row128 = lax.broadcasted_iota(jnp.int32, (128, 128), 0)
    col128 = lax.broadcasted_iota(jnp.int32, (128, 128), 1)
    same = (row128 // 64) == (col128 // 64)
    earlier = jnp.where(same & (row128 < col128), 1.0, 0.0).astype(bf16)
    block = jnp.where(same, 1.0, 0.0).astype(bf16)
    row256 = lax.broadcasted_iota(jnp.int32, (256, 256), 0)
    col256 = lax.broadcasted_iota(jnp.int32, (256, 256), 1)
    above = jnp.where(((row256 % 16) == (col256 % 16)) & (col256 < row256 - row256 % 16), 1.0, 0.0)
    lists_before = jnp.dot(above.astype(bf16), onehot16, preferred_element_type=f32).astype(bf16)
    count = jnp.dot(onehot16, earlier, preferred_element_type=f32)
    count = count + jnp.dot(lists_before, block, preferred_element_type=f32)
    slot = jnp.sum((onehot * count).reshape(16, 16, 128), 1)

    target = jnp.where(lane16 < 64, slot, slot + 128.0)
    high = (payload >> 5).astype(f32)
    low = (payload & 31).astype(f32)
    sub256 = lax.broadcasted_iota(jnp.int32, (256, 128), 0).astype(f32)
    pad = jnp.zeros((96, 128), f32)
    table = jnp.zeros((256, 128), f32)
    for r in range(16):
        here = jnp.where(target[r : r + 1, :] == sub256, 1.0, 0.0).astype(bf16)
        digit = jnp.concatenate([marks[r] * high[r : r + 1, :], marks[r] * low[r : r + 1, :], pad], 0)
        table = table + lax.dot_general(here, digit.astype(bf16), NT, preferred_element_type=f32)
    table = jnp.transpose(table)
    table = table[:16] * 32.0 + table[16:32]
    first_row = lax.broadcasted_iota(jnp.int32, (8, 128), 0) == 0
    for k in range(16):
        msg[k] = jnp.where(first_row, table[k : k + 1, :128], table[k : k + 1, 128:])
    got[0] = msg[0]

    wide = lax.broadcasted_iota(jnp.int32, (16, 128), 1).astype(f32)
    mix = jnp.zeros((16, 128), f32)
    for j in range(4):
        place = rel[:, 64 + j : 65 + j] * 8.0 + slot[:, 64 + j : 65 + j]
        mix = mix + jnp.where(place == wide, 1.0, 0.0)
    pick = jnp.transpose(jnp.concatenate([mix, jnp.zeros((112, 128), f32)], 0)).astype(bf16)
    padded = jnp.concatenate([qry[...], jnp.zeros((112, D), bf16)], 0)
    picked = jnp.dot(pick, padded, preferred_element_type=f32)

    def fold(rows):
        return jnp.concatenate([rows[:, :512], rows[:, 512:]], 0).astype(bf16)

    for k in range(16):
        ask[k] = fold(picked[k * 8 : (k + 1) * 8])
    asked[0] = ask[0]

    pl.semaphore_wait(barrier, 19)

    def remote(src, dst, sems, k):
        copy = pltpu.make_async_remote_copy(
            src_ref=src,
            dst_ref=dst,
            send_sem=sems.at[0, k],
            recv_sem=sems.at[1, inverse(k)],
            device_id=peer(k),
            device_id_type=MESH,
        )
        copy.start()
        return copy

    steps = [dy * 4 + dx * 2 for dy, dx in ORDER]
    pairs = [k for first in steps for k in (first, first + 1) if k]
    m_copy = {k: remote(msg.at[k], got.at[inverse(k)], msem, k) for k in pairs}
    q_copy = {k: remote(ask.at[k], asked.at[inverse(k)], qsem, k) for k in pairs}

    w_in = (wq_i, wo_i, wu_i, wd_i)
    w_out = (wq.at[1], wo.at[1], wu.at[1], wd.at[1])

    def share(refs, unit, zz, cc, half=None):
        n, j = UNITS[unit]
        rows = ROWS[n]
        start = (zz * 2 + cc) * rows
        if half is not None:
            rows = rows // 2
            start = start + half * rows
        part = pl.ds(pl.multiple_of(start, 32), rows)
        return refs[n].at[j, part, :] if n == 0 else refs[n].at[part, :]

    def push(src, dst, unit, s, device):
        copy = pltpu.make_async_remote_copy(
            src_ref=src,
            dst_ref=dst,
            send_sem=wsend.at[unit, s],
            recv_sem=wrecv.at[unit, s],
            device_id=device,
            device_id_type=MESH,
        )
        copy.start()
        return copy

    started = {}
    for u in range(6):
        started[u, 0] = push(share(w_in, u, z, c), share(w_out, u, z, c), u, 0, partner)
    own_copies = []
    for n, here in enumerate((wq, wo, wu, wd)):
        own_copies.append(pltpu.make_async_copy(w_in[n], here.at[0], lsem.at[n]))
        own_copies[n].start()

    def relay(u, stage):
        def put(s, zz, half, device):
            ref = share(w_out, u, zz, c, half)
            started[u, s] = push(ref, ref, u, s, device)

        zm, zp, zo = (z + 3) % 4, (z + 1) % 4, (z + 2) % 4
        if stage == 0:
            started[u, 0].wait_recv()
            put(1, z, None, z_up)
            put(2, z, None, z_down)
            if u >= 4:
                put(3, z, None, z_across)
            put(5, z, None, peer(1))
        elif u >= 4:
            for s, zz in ((1, zm), (2, zp), (3, zo)):
                started[u, s].wait_recv()
                put(s + 5, zz, None, peer(1))
        elif stage == 1:
            started[u, 1].wait_recv()
            put(3, zm, 0, z_up)
            put(6, zm, None, peer(1))
            started[u, 2].wait_recv()
            put(4, zp, 1, z_down)
            put(7, zp, None, peer(1))
        else:
            started[u, 3].wait_recv()
            started[u, 4].wait_recv()
            put(8, zo, None, peer(1))

    def landed(*units):
        for u in units:
            for s in range(5, 9):
                started[u, s].wait_recv()

    flat = rel * 128.0 + slot
    eye = row128 == col128
    for r in range(16):
        column = jnp.sum(jnp.where(eye[:64], flat[r : r + 1, :], 0.0), 1, keepdims=True)
        flatcol[r * 64 : (r + 1) * 64, :] = jnp.broadcast_to(column, (64, 128))

    def probes():
        eye8 = eye[:8]
        for k in range(16):
            column = jnp.sum(jnp.where(eye8, got[k, 1:2, :], 0.0), 1, keepdims=True)
            codes[k * 8 : (k + 1) * 8, :] = jnp.broadcast_to(column, (8, 128))
        for k in pairs:
            q_copy[k].wait_recv()
        cluster = codes[:, 0:1].astype(jnp.int32) & 3
        rows16 = asked[...].reshape(256, 512)

        def score_step(n, carry):
            rows = pl.ds(pl.multiple_of(n * 512, 512), 512)
            left = lax.dot_general(rows16, psg[rows, :512], NT, preferred_element_type=f32)
            right = lax.dot_general(rows16, psg[rows, 512:], NT, preferred_element_type=f32)
            s = left.reshape(16, 2, 8, 512)[:, 0] + right.reshape(16, 2, 8, 512)[:, 1]
            score[:, rows] = jnp.where(cluster == n, s.reshape(128, 512) * (D ** (-0.5)), -1e30)
            return carry

        lax.fori_loop(0, 4, score_step, 0)
        peak = jnp.max(score[...], 1, keepdims=True)
        expo = jnp.exp(score[...] - peak)
        weights = (expo / jnp.sum(expo, 1, keepdims=True)).astype(bf16)
        pooled = jnp.dot(weights, psg[...], preferred_element_type=f32)
        for k in range(16):
            rows = fold(pooled[k * 8 : (k + 1) * 8])
            if k:
                pool[k] = rows
            else:
                prow[0] = rows
        return {k: remote(pool.at[k], prow.at[inverse(k)], osem, k) for k in pairs}

    load.wait()
    r_copy = {}
    waited = set()
    lanes = lax.broadcasted_iota(jnp.int32, (128, 2048), 1).astype(f32)
    for number, first in enumerate(steps):
        for k in (first, first + 1):
            if k and k not in waited:
                m_copy[inverse(k)].wait_recv()
                waited.add(k)
            column = jnp.sum(jnp.where(eye, got[k, 0:1, :], 0.0), 1, keepdims=True)
            hot[(k % 2) * 128 : (k % 2 + 1) * 128, :] = jnp.where(column == lanes, 1.0, 0.0).astype(bf16)

        def gather(n, carry, first=first):
            cols = pl.ds(pl.multiple_of(n * 256, 256), 256)
            rows = jnp.dot(hot[...], psg[:, cols], preferred_element_type=f32).astype(bf16)
            if first:
                reply_vc[first * 128 : (first + 1) * 128, cols] = rows[:128]
            else:
                back[0, :, cols] = rows[:128]
            reply_vc[(first + 1) * 128 : (first + 2) * 128, cols] = rows[128:]
            return carry

        lax.fori_loop(0, 4, gather, 0)
        for k in (first, first + 1):
            if k:
                r_copy[k] = remote(reply_vc.at[k * 128 : (k + 1) * 128], back.at[inverse(k)], rsem, k)
        if number == 2:
            for k in pairs:
                if k not in waited:
                    m_copy[inverse(k)].wait_recv()
                    waited.add(k)
            p_copy = probes()
        for u, stage in PLAN.get(number, ()):
            relay(u, stage)

    def assemble(dy, fresh):
        for k in range(dy * 4, dy * 4 + 4):
            if k:
                r_copy[inverse(k)].wait_recv()
        wide = (lax.broadcasted_iota(jnp.int32, (256, 512), 1) + dy * 512).astype(f32)

        def part(n, carry):
            rows = pl.ds(pl.multiple_of(n * 256, 256), 256)
            place = jnp.concatenate([flatcol[rows, :]] * 4, 1)
            mark = jnp.where(place == wide, 1.0, 0.0).astype(bf16)
            values = back[dy * 4 : dy * 4 + 4].reshape(512, D)
            found = jnp.dot(mark, values, preferred_element_type=f32).astype(bf16)
            tok[rows, :] = found if fresh else tok[rows, :] + found
            return carry

        lax.fori_loop(0, 4, part, 0)

    relay(3, 2)
    assemble(2, True)
    relay(5, 0)
    for k in pairs:
        p_copy[k].wait_recv()
    wide = lax.broadcasted_iota(jnp.int32, (16, 256), 1).astype(f32)
    halves = []
    for half in range(2):
        mix = jnp.zeros((16, 256), f32)
        for j in range(4):
            place = rel[:, 64 + j : 65 + j] * 16.0 + slot[:, 64 + j : 65 + j] + half * 8.0
            mix = mix + jnp.where(place == wide, 1.0, 0.0)
        halves.append(
            jnp.dot(mix.astype(bf16), prow[...].reshape(256, 512), preferred_element_type=f32)
        )
    summed = jnp.concatenate(halves, 1)
    tok[N_C:, :] = (qry[...].astype(f32) + summed * 0.25).astype(bf16)
    assemble(1, False)
    assemble(3, False)
    assemble(0, False)
    for copy in r_copy.values():
        copy.wait_send()

    for i in range(2):
        if i == 0:
            own_copies[0].wait()
        else:
            landed(0, 1, 2)
        def qkv_step(n,carry):
            col=pl.ds(pl.multiple_of(n*256,256),256)
            ocol=pl.ds(pl.multiple_of(i*512+n*256,256),256)
            for j,ref in enumerate((qs,ks,vs)):
                r=jnp.dot(tok[...],wq[i,j,:,col],preferred_element_type=f32)
                if j==0: r=r*0.125
                ref[:,ocol]=r.astype(bf16)
            return carry
        lax.fori_loop(0,2,qkv_step,0)
    relay(4, 2)
    vl[...]=vs[N_C:,:].astype(f32)
    ctxl[...]=jnp.zeros_like(ctxl)
    lane=lax.broadcasted_iota(jnp.int32,(64,256),1)//64
    ones_bd=(lax.broadcasted_iota(jnp.int32,(256,256),0)//64==lax.broadcasted_iota(jnp.int32,(256,256),1)//64).astype(bf16)
    bd_mask=lax.broadcasted_iota(jnp.int32,(256,256),0)//64==lax.broadcasted_iota(jnp.int32,(256,256),1)//64
    low=lax.broadcasted_iota(jnp.int32,(80,128),1)<64
    rowid=lax.broadcasted_iota(jnp.int32,(16,256),0)
    def bd(x):
        return jnp.concatenate([jnp.where(lane==h,x,jnp.zeros_like(x)) for h in range(4)],0)
    lead_mask=lax.broadcasted_iota(jnp.int32,(16,256),1)//64
    for j in range(4):
        cs=slice(j*256,(j+1)*256)
        kj=ks[N_C:,cs]
        rows_hl=jnp.concatenate([jnp.where(lead_mask==h,kj,jnp.zeros_like(kj)) for h in range(4)]+[jnp.zeros((64,256),bf16)],0)
        sl[:,j*128:(j+1)*128]=lax.dot_general(qs[:,cs],rows_hl,NT,preferred_element_type=f32)
    erow=lax.broadcasted_iota(jnp.int32,(256,256),0)%128
    ecol=lax.broadcasted_iota(jnp.int32,(256,256),1)
    def att(g,carry):
        rows=pl.ds(pl.multiple_of(g*64,64),64)
        expand=jnp.where(erow==(ecol//64)*16+g,1.0,0.0).astype(bf16)
        parts=[]
        for j in range(4):
            x=jnp.concatenate([sl[rows,j*128:(j+1)*128],sl[N_C:,j*128:(j+1)*128]],0)
            hi=x.astype(bf16)
            parts.append(jnp.concatenate([hi,(x-hi.astype(f32)).astype(bf16)],1))
        SLall=jnp.dot(jnp.concatenate(parts,0),expand,preferred_element_type=f32)
        es=[];els=[]
        for j in range(4):
            cs=slice(j*256,(j+1)*256)
            Q=jnp.concatenate([qs[rows,cs],qs[N_C:,cs]],0)
            kt=jnp.transpose(jnp.concatenate([ks[rows,cs],ks[rows,cs]],0))
            kt=jnp.concatenate([kt,kt],1)
            S=jnp.dot(Q,jnp.where(bd_mask,kt,jnp.zeros_like(kt)),preferred_element_type=f32)
            SL=SLall[j*80:(j+1)*80]
            ms=[]
            for b in range(2):
                X=S[:,b*128:(b+1)*128]
                mA=jnp.max(jnp.where(low,X,-jnp.inf),1,keepdims=True)
                mB=jnp.max(jnp.where(low,-jnp.inf,X),1,keepdims=True)
                ms.append(jnp.where(low,mA,mB))
            m=jnp.maximum(jnp.concatenate(ms,1),SL)
            es.append(jnp.exp(S-m).astype(bf16)); els.append(jnp.exp(SL-m))
        den=jnp.dot(jnp.concatenate(es,0),ones_bd,preferred_element_type=f32)
        for j in range(4):
            cs=slice(j*256,(j+1)*256)
            pv=jnp.dot(es[j],bd(vs[rows,cs]),preferred_element_type=f32)
            c=(pv+els[j]*vl[pl.ds(g,1),cs])/(den[j*80:(j+1)*80]+els[j])
            ctx[rows,cs]=c[:64].astype(bf16)
            ctxl[:,cs]+=jnp.where(rowid==g,c[64:],0.0)
        return carry
    lax.fori_loop(0, 16, att, 0, unroll=4)
    ctx[N_C:,:]=ctxl[...].astype(bf16)
    relay(5, 2)
    own_copies[1].wait()
    landed(3)
    def outp(rows,n):
        a=jnp.dot(ctx[rows,:512],wo[0],preferred_element_type=f32)+jnp.dot(ctx[rows,512:],wo[1],preferred_element_type=f32)
        return norm(tok[rows,:].astype(f32)+a,g1[...]).astype(bf16).astype(f32)
    def put(g,y):
        for c in range(8): acc[c,pl.ds(16+g,64,stride=16),:]=y[:,c*128:(c+1)*128]
    def outc(i,carry):
        h=outp(pl.ds(pl.multiple_of(i*256,256),256),256)
        for l in range(4):
            put(i*4+l,h[l*64:(l+1)*64])
        return carry
    lax.fori_loop(0,3,outc,0)
    h=outp(slice(768,1040),272)
    for l in range(4):
        put(12+l,h[l*64:(l+1)*64])
    for c in range(8): acc[c,0:16,:]=h[256:,c*128:(c+1)*128]
    own_copies[2].wait()
    own_copies[3].wait()
    landed(4, 5)
    def ffn(r,carry):
        rows=pl.ds(pl.multiple_of(r*208,16),208)
        t=jnp.concatenate([acc[c,rows,:] for c in range(8)],1)
        x=t.astype(bf16)
        acts=[]
        for i in range(2):
            for n in range(4):
                u=jnp.dot(x,wu[i,:,n*512:(n+1)*512],preferred_element_type=f32)
                acts.append(gelu(u).astype(bf16))
        for i in range(2):
            t=t+jnp.dot(jnp.concatenate(acts[i*4:(i+1)*4],1),wd[i],preferred_element_type=f32)
        tok[rows,:]=norm(t,g2[...]).astype(bf16)
        pltpu.make_async_copy(tok.at[rows],out.at[rows],fsem.at[r]).start()
        return carry
    lax.fori_loop(0,5,ffn,0)
    for r in range(5):
        rows=slice(r*208,(r+1)*208)
        pltpu.make_async_copy(tok.at[rows],out.at[rows],fsem.at[r]).wait()
    for copies in (m_copy, q_copy, p_copy, started):
        for copy in copies.values():
            copy.wait_send()


def whole(p_own, p_row, o_own, o_clu, qry, passages, wq, wo, wu, wd, g1, g2):
    vmem = pl.BlockSpec(memory_space=pltpu.VMEM)
    hbm = pl.BlockSpec(memory_space=pl.ANY)
    dma = pltpu.SemaphoreType.DMA
    return pl.pallas_call(
        whole_kernel,
        out_shape=jax.ShapeDtypeStruct((N_TOK, D), bf16),
        in_specs=[vmem] * 5 + [hbm] * 5 + [vmem, vmem],
        out_specs=hbm,
        scratch_shapes=[
            pltpu.VMEM((2, 3, D, 512), bf16),
            pltpu.VMEM((2, 512, D), bf16),
            pltpu.VMEM((2, D, 2048), bf16),
            pltpu.VMEM((2, 2048, D), bf16),
            pltpu.VMEM((N_TOK, D), bf16),
            pltpu.VMEM((2 * N_TOK, D), bf16),
            pltpu.VMEM((2 * N_TOK, D), bf16),
            pltpu.VMEM((N_TOK, 512), f32),
            pltpu.VMEM((16, D), f32),
            pltpu.VMEM((16, D), f32),
            pltpu.VMEM((8, N_TOK, 128), f32),
            pltpu.VMEM((16, 16, 512), bf16),
            pltpu.VMEM((16, 16, 512), bf16),
            pltpu.VMEM((16, 8, 128), f32),
            pltpu.VMEM((16, 8, 128), f32),
            pltpu.VMEM((256, 2048), bf16),
            pltpu.VMEM((16, 128, D), bf16),
            pltpu.VMEM((128, 128), f32),
            pltpu.VMEM((128, PASS_DEV), f32),
            pltpu.VMEM((16, 16, 512), bf16),
            pltpu.VMEM((16, 16, 512), bf16),
            pltpu.VMEM((N_C, 128), f32),
            dma(()),
            dma((2, 16)),
            dma((2, 16)),
            dma((2, 16)),
            dma((2, 16)),
            dma((6, 9)),
            dma((6, 9)),
            dma((4,)),
            dma((5,)),
            pltpu.VMEM((2, 128, 128), f32),
            pltpu.VMEM((16, 128), jnp.int32),
            pltpu.VMEM((16, 128), jnp.int32),
        ],
        compiler_params=pltpu.CompilerParams(
            collective_id=0, has_side_effects=True, vmem_limit_bytes=62 * 2**20
        ),
        cost_estimate=pl.CostEstimate(flops=2**35, bytes_accessed=50 * 2**20, transcendentals=0),
        name="whole",
    )(p_own, p_row, o_own, o_clu, qry, passages, wq, wo, wu, wd, g1, g2)


def on_device(
    queries,
    passages,
    probe_owner,
    probe_cluster,
    pair_owner,
    pair_row,
    w_qkv,
    w_out,
    w_up,
    w_down,
    gain_one,
    gain_two,
):
    wq = jnp.transpose(w_qkv, (1, 0, 2))
    rows = whole(
        jnp.transpose(pair_owner, (0, 2, 1)), pair_row, probe_owner.T, probe_cluster.T, queries, passages, wq, w_out, w_up, w_down, gain_one[None, :], gain_two[None, :]
    )
    return jnp.transpose(rows.reshape(65, 16, D), (1, 0, 2))


def solution(mesh):
    rows = P(("index", "rep", "tp"), None)
    lists = P(("index", "rep", "tp"), None, None)
    in_specs = (
        rows,
        P("index", None),
        rows,
        rows,
        lists,
        rows,
        P(None, None, "tp"),
        P("tp", None),
        P(None, "tp"),
        P("tp", None),
        P(),
        P(),
    )
    return jax.shard_map(
        on_device, mesh=mesh, in_specs=in_specs, out_specs=lists, check_vma=False
    )
```
